128 devices in a mesh: ctx: 32 (over y, z, core), tp: 4 (over x).
Axes of the slice: x: 4, y: 4, z: 4, core: 2. Of those that a mesh axis runs over, the one named last changes fastest.
Arguments:
- query_proj: bfloat16 [4096, 8192], P('ctx', 'tp'), may hold values from -6 to 6
- key_proj: bfloat16 [4096, 8192], P('ctx', 'tp'), may hold values from -6 to 6
- value_proj: bfloat16 [4096, 8192], P('ctx', 'tp'), may hold values from -6 to 6
- short_filter: float32 [3, 3, 8192], P(None, None, 'tp'), may hold values from -3 to 3
- skip_gain: float32 [8192], P('tp'), may hold values from -4 to 4
- pole_rates: float32 [8192, 16], P('tp'), as said below
- pole_residues: float32 [8192, 16], P('tp'), as said below
Outputs:
- mixer_out: bfloat16 [4096, 8192], P('ctx', 'tp')
The draws below stay inside these ranges and needn't reach their ends.
Inputs may be any that keep to these rules, and one draw needn't show every extreme that they name: `pole_rates`: every decay rate lies between 0.3 / 4096 and 1 / 30. `pole_residues`: residues are real numbers of either sign.
All inputs are finite; a program needn't handle non-finite values.
Results may differ from the reference program's by a relative error of at most 0.02.
Values may be sent and summed in bfloat16 or wider, within the bound.
No kernel may reach another device: no remote copies, remote signals or barrier semaphores. Data moves between devices by JAX's collectives and lax.ppermute only.
A program may use at most 64 MiB of HBM per device.

```python
import math
import jax
import jax.numpy as jnp
from jax import lax

D = 8192
POLES = 16
SEQ = 4096


def draw_pole_rates(key, part):
    key = jax.random.fold_in(key, 11)
    uniform_part = jax.random.uniform(key, (D, POLES), jnp.float32)
    low_end = math.log(0.3 / SEQ)
    high_end = math.log(1.0 / 30.0)
    return jnp.exp(low_end + uniform_part * (high_end - low_end))


def draw_pole_residues(key, part):
    key = jax.random.fold_in(key, 23)
    return jax.random.normal(key, (D, POLES), jnp.float32) * (0.5 / math.sqrt(SEQ))


def steps_of(own_key, dims, shards, smallest, top_value):
    def one(dim, blocks):
        heights = jax.random.uniform(jax.random.fold_in(jax.random.fold_in(own_key, 6), dim), (blocks,), jnp.float32, smallest / len(shards), top_value / len(shards))
        return jnp.repeat(jnp.exp(heights), dims[dim] // blocks).reshape((-1,) + (1,) * (len(dims) - dim - 1))

    level = one(*shards[0])
    for cut in shards[1:]:
        level = level * one(*cut)
    return level


def noise(own_key, shape, scale, limit, split=(), kind=jnp.bfloat16):
    level = steps_of(own_key, shape, split, -0.22, 0.18) if split else 1.0
    entries = jax.random.normal(own_key, shape, jnp.float32) * scale * level
    return jnp.minimum(jnp.maximum(entries, -limit), limit).astype(kind)


def setup_inputs(seed: int = 0) -> dict:
    splits = jax.random.split(jax.random.key(seed), 8)
    query_proj = noise(splits[0], (SEQ, D), 1.0, 6.0, ((0, 32), (1, 4)))
    key_proj = noise(splits[1], (SEQ, D), 1.0, 6.0, ((0, 32), (1, 4)))
    value_proj = noise(splits[2], (SEQ, D), 1.0, 6.0, ((0, 32), (1, 4)))
    short_filter = noise(splits[3], (3, 3, D), 0.6, 3.0, ((2, 4),), jnp.float32)
    skip_gain = noise(splits[4], (D,), 1.0, 4.0, ((0, 4),), jnp.float32)
    pole_rates = draw_pole_rates(jax.random.fold_in(splits[7], 71), 0)
    pole_residues = draw_pole_residues(jax.random.fold_in(splits[7], 71), 0)
    return {"query_proj": query_proj, "key_proj": key_proj, "value_proj": value_proj, "short_filter": short_filter, "skip_gain": skip_gain, "pole_rates": pole_rates, "pole_residues": pole_residues}


def featurize(signal, tap_weights):
    values = signal.astype(jnp.float32)
    padded = jnp.pad(values, ((2, 0), (0, 0)))
    output_values = tap_weights[0] * values + tap_weights[1] * padded[1:-1] + tap_weights[2] * padded[:-2]
    return output_values.astype(jnp.bfloat16)


def reference(query_proj, key_proj, value_proj, short_filter, skip_gain, pole_rates, pole_residues):
    query_feat = featurize(query_proj, short_filter[0])
    key_feat = featurize(key_proj, short_filter[1])
    value_feat = featurize(value_proj, short_filter[2])
    product = (key_feat.astype(jnp.float32) * value_feat.astype(jnp.float32)).astype(jnp.bfloat16)
    positions = jnp.arange(SEQ).astype(jnp.float32)
    column_blocks = product.T.reshape(D // 128, 128, SEQ)
    rate_blocks = pole_rates.reshape(D // 128, 128, POLES)
    residue_blocks = pole_residues.reshape(D // 128, 128, POLES)

    def one_block(pieces):
        columns, rate_part, residue_part = pieces
        decays = jnp.exp(-rate_part[:, :, None] * positions[None, None, :])
        kernel = jnp.sum(residue_part[:, :, None] * decays, axis=1)
        spectrum = jnp.fft.rfft(columns.astype(jnp.float32), n=2 * SEQ, axis=-1) * jnp.fft.rfft(kernel, n=2 * SEQ, axis=-1)
        return jnp.fft.irfft(spectrum, n=2 * SEQ, axis=-1)[:, :SEQ].astype(jnp.bfloat16)

    convolved = lax.map(one_block, (column_blocks, rate_blocks, residue_blocks)).reshape(D, SEQ).T
    mixer_out = query_feat.astype(jnp.float32) * (convolved.astype(jnp.float32) + skip_gain * product.astype(jnp.float32))
    return mixer_out.astype(jnp.bfloat16)
```

```python
import functools

import jax
import jax.numpy as jnp
import numpy as np
from jax import lax
from jax.experimental import pallas as pl
from jax.experimental.pallas import tpu as pltpu
from jax.sharding import PartitionSpec as P

import ml_dtypes

RATE_MIN, RATE_MAX = 0.3 / 4096, 1.0 / 30.0
SHIFT = 1.2e-3
NODES = 24
RANK = 8
PAD = 80
F32 = jnp.float32
BF16 = jnp.bfloat16


def split_np(values):
    high = values.astype(np.float32).astype(ml_dtypes.bfloat16)
    low = (values - high.astype(np.float64)).astype(np.float32).astype(ml_dtypes.bfloat16)
    return high, low


def log_range():
    low, high = np.log(RATE_MIN + SHIFT), np.log(RATE_MAX + SHIFT)
    return (low + high) / 2, (high - low) / 2


@functools.lru_cache(maxsize=None)
def tables(block, devices):
    mid, half = log_range()
    order = np.arange(NODES)
    node_x = np.cos((2 * order + 1) * np.pi / (2 * NODES))
    nodes = np.exp(mid + half * node_x) - SHIFT
    weights = np.full(NODES, 2.0 / NODES)
    weights[0] = 1.0 / NODES
    to_nodes = np.cos(order[None, :] * np.arccos(node_x)[:, None]) * weights[None, :]

    lags = np.arange(block)
    rates = np.linspace(RATE_MIN, RATE_MAX, 1500)
    basis = np.linalg.svd(np.exp(-np.outer(rates, lags)), full_matrices=False)[2][:RANK]
    shares = np.exp(-np.outer(nodes, lags)) @ basis.T
    mix = np.concatenate([to_nodes, shares.T @ to_nodes], 0).astype(np.float32)

    lag = lags[:, None] - lags[None, :]
    toeplitz = np.where(lag >= 0, basis[:, np.maximum(lag, 0)], 0.0).reshape(RANK * block, block)
    toeplitz = np.concatenate(split_np(toeplitz), 1)
    reverse = basis[:, ::-1]
    moment = np.concatenate(split_np(reverse), 1)
    first = np.zeros((RANK, 128), np.float32)
    first[:, :2] = reverse[:, :2]

    gap = np.arange(devices)[:, None] - 1 - np.arange(devices)[None, :]
    decay = np.where(
        gap[:, None, :] >= 0, np.exp(-nodes[None, :, None] * block * np.maximum(gap, 0)[:, None, :]), 0.0
    )
    carry = (decay[:, :, :, None] * shares[None, :, None, :]).reshape(devices, NODES, devices * RANK)
    carry = np.concatenate(split_np(carry), 1).reshape(devices * 2 * NODES, devices * RANK)

    parts = [np.exp(-np.outer(lags + 1 - by, nodes)) * (lags >= by - 1)[:, None] for by in (0, 1, 2)]
    spread = np.concatenate(parts + [np.zeros((block, PAD - 3 * NODES))], 1)
    high, low = split_np(spread)
    spread = np.concatenate([high, low, high], 1)
    return mix, toeplitz, moment, first, carry, spread


def split(values):
    high = values.astype(BF16)
    return high, (values - high.astype(F32)).astype(BF16)


def dot(left, right):
    return jnp.dot(left, right, preferred_element_type=F32)


def taps_of(values, taps):
    return taps[0:1] * values + taps[1:2] * pltpu.roll(values, 1, 0) + taps[2:3] * pltpu.roll(values, 2, 0)


def rounded(values):
    return values.astype(BF16).astype(F32)


def local_kernel(k_ref, v_ref, taps_ref, rates_ref, residues_ref, mix_ref, toeplitz_ref, moment_ref,
                 product_ref, local_ref, part_ref, weight_ref, cheb_ref):
    mid, half = log_range()
    x = (jnp.log(rates_ref[...] + SHIFT) - mid) * (1.0 / half)
    before = residues_ref[...]
    now = before * x
    cheb_ref[0:1] = jnp.sum(before, 0, keepdims=True)
    cheb_ref[1:2] = jnp.sum(now, 0, keepdims=True)
    twice = 2.0 * x
    for order in range(2, NODES):
        before, now = now, twice * now - before
        cheb_ref[order : order + 1] = jnp.sum(now, 0, keepdims=True)
    mixed = jnp.dot(mix_ref[...], cheb_ref[...], preferred_element_type=F32, precision=lax.Precision.HIGHEST)
    weight_ref[...] = mixed[:NODES]

    key_feat = rounded(taps_of(k_ref[...].astype(F32), taps_ref[1]))
    value_feat = rounded(taps_of(v_ref[...].astype(F32), taps_ref[2]))
    product = key_feat * value_feat
    row = lax.broadcasted_iota(jnp.int32, product.shape, 0)
    product = jnp.where(row < 2, 0.0, product).astype(BF16)
    product_ref[...] = product
    block = product.shape[0]
    twin = jnp.concatenate([product, product], 0)
    part_ref[...] = dot(moment_ref[...], twin)
    for half_idx in range(product.shape[1] // 256):
        cols = slice(half_idx * 256, half_idx * 256 + 256)
        total = None
        for k in range(RANK):
            term = mixed[NODES + k : NODES + k + 1, cols] * dot(
                toeplitz_ref[k * block : (k + 1) * block], twin[:, cols]
            )
            total = term if total is None else total + term
        local_ref[:, cols] = total


def edge_kernel(k_ref, v_ref, edge_ref, taps_ref, part_ref, first_ref, sent_ref, rows_ref):
    edge = edge_ref[...].astype(F32)

    def two_rows(values, tail, taps):
        row0 = taps[0:1] * values[0:1] + taps[1:2] * tail[1:2] + taps[2:3] * tail[0:1]
        row1 = taps[0:1] * values[1:2] + taps[1:2] * values[0:1] + taps[2:3] * tail[1:2]
        return rounded(row0), rounded(row1)

    key0, key1 = two_rows(k_ref[...].astype(F32), edge[2:4], taps_ref[1])
    value0, value1 = two_rows(v_ref[...].astype(F32), edge[4:6], taps_ref[2])
    row0, row1 = rounded(key0 * value0), rounded(key1 * value1)
    rows_ref[...] = jnp.concatenate([row0, row1, jnp.zeros((6, row0.shape[1]), F32)], 0)
    first = first_ref[...]
    whole = part_ref[...] + first[:, 0:1] * row0 + first[:, 1:2] * row1
    copies = 16 // RANK
    pair = jnp.concatenate([whole] * copies, 0).astype(BF16)
    for idx in range(sent_ref.shape[0] // 16):
        sent_ref[idx * 16 : idx * 16 + 16] = pair


def out_kernel(idx_ref, q_ref, edge_ref, taps_ref, skip_ref, product_ref, local_ref, rows_ref, weight_ref,
               got_ref, carry_ref, spread_ref, out_ref):
    state = dot(carry_ref[...], got_ref[...])
    state = state[:NODES] + state[NODES:]
    weight = weight_ref[...]
    row0, row1 = rows_ref[0:1], rows_ref[1:2]
    columns = weight.shape[1]
    stacked = jnp.concatenate(
        [weight * state, weight * row0, weight * row1, jnp.zeros((PAD - 3 * NODES, columns), F32)], 0
    )
    high, low = split(stacked)
    convolved = local_ref[...] + dot(spread_ref[...], jnp.concatenate([high, high, low], 0))

    values = q_ref[...].astype(F32)
    edge = edge_ref[...].astype(F32)
    taps = taps_ref[0]
    row = lax.broadcasted_iota(jnp.int32, values.shape, 0)
    one = jnp.where(row == 0, edge[1:2], pltpu.roll(values, 1, 0))
    two = jnp.where(row == 0, edge[0:1], jnp.where(row == 1, edge[1:2], pltpu.roll(values, 2, 0)))
    query_feat = rounded(taps[0:1] * values + taps[1:2] * one + taps[2:3] * two)
    product = product_ref[...].astype(F32)
    product = jnp.where(row == 0, row0, jnp.where(row == 1, row1, product))
    out_ref[...] = (query_feat * (rounded(convolved) + skip_ref[...] * product)).astype(BF16)


def on_device(query_proj, key_proj, value_proj, short_filter, skip_gain, pole_rates, pole_residues):
    block, channels = query_proj.shape
    devices = lax.axis_size("ctx")
    mix, toeplitz, moment, first, carry, spread = tables(block, devices)
    width = min(512, channels)
    grid = (channels // width,)

    def cols(rows):
        return pl.BlockSpec((rows, width), lambda i, *_: (0, i))

    def fixed(array):
        return pl.BlockSpec(array.shape, lambda i, *_: (0,) * array.ndim)

    taps_spec = pl.BlockSpec((3, 3, width), lambda i, *_: (0, 0, i))
    params = pltpu.CompilerParams(vmem_limit_bytes=48 * 1024 * 1024)

    tails = jnp.concatenate([query_proj[-2:], key_proj[-2:], value_proj[-2:]], 0)
    edge = lax.ppermute(tails, "ctx", [(i, i + 1) for i in range(devices - 1)])

    poles = pole_rates.shape[1]
    product, local, part, weight = pl.pallas_call(
        local_kernel,
        grid=grid,
        in_specs=[cols(block), cols(block), taps_spec, cols(poles), cols(poles), fixed(mix), fixed(toeplitz),
                  fixed(moment)],
        out_specs=[cols(block), cols(block), cols(RANK), cols(NODES)],
        out_shape=[
            jax.ShapeDtypeStruct((block, channels), BF16),
            jax.ShapeDtypeStruct((block, channels), F32),
            jax.ShapeDtypeStruct((RANK, channels), F32),
            jax.ShapeDtypeStruct((NODES, channels), F32),
        ],
        scratch_shapes=[pltpu.VMEM((NODES, width), F32)],
        compiler_params=params,
        cost_estimate=pl.CostEstimate(
            flops=2 * toeplitz.size * channels, bytes_accessed=4 * block * channels * 3, transcendentals=0
        ),
        name="local",
    )(key_proj, value_proj, short_filter, pole_rates.T, pole_residues.T, jnp.asarray(mix),
      jnp.asarray(toeplitz), jnp.asarray(moment))

    sent, rows = pl.pallas_call(
        edge_kernel,
        grid=grid,
        in_specs=[cols(16), cols(16), cols(6), taps_spec, cols(RANK), fixed(first)],
        out_specs=[cols(devices * RANK), cols(8)],
        out_shape=[
            jax.ShapeDtypeStruct((devices * RANK, channels), BF16),
            jax.ShapeDtypeStruct((8, channels), F32),
        ],
        compiler_params=params,
        name="edge",
    )(key_proj, value_proj, edge, short_filter, part, jnp.asarray(first))

    got = lax.all_to_all(sent, "ctx", 0, 0, tiled=True)

    place = lax.axis_index("ctx").astype(jnp.int32).reshape(1)
    return pl.pallas_call(
        out_kernel,
        grid_spec=pltpu.PrefetchScalarGridSpec(
            num_scalar_prefetch=1,
            grid=grid,
            in_specs=[
                cols(block), cols(6), taps_spec, cols(1), cols(block), cols(block), cols(8), cols(NODES),
                cols(devices * RANK),
                pl.BlockSpec((2 * NODES, devices * RANK), lambda i, idx: (idx[0], 0)),
                fixed(spread),
            ],
            out_specs=cols(block),
        ),
        out_shape=jax.ShapeDtypeStruct((block, channels), BF16),
        compiler_params=params,
        name="output",
    )(place, query_proj, edge, short_filter, skip_gain.reshape(1, -1), product, local, rows, weight, got,
      jnp.asarray(carry), jnp.asarray(spread))


def solution(mesh):
    placed = (
        P("ctx", "tp"),
        P("ctx", "tp"),
        P("ctx", "tp"),
        P(None, None, "tp"),
        P("tp"),
        P("tp", None),
        P("tp", None),
    )
    return jax.shard_map(
        on_device, mesh=mesh, in_specs=placed, out_specs=P("ctx", "tp"), check_vma=False
    )
```

```python
import functools

import jax
import jax.numpy as jnp
import ml_dtypes
import numpy as np
from jax import lax
from jax.experimental import pallas as pl
from jax.experimental.pallas import tpu as pltpu
from jax.sharding import PartitionSpec as P

RATE_MIN, RATE_MAX = 0.3 / 4096, 1.0 / 30.0
SHIFT = 1.2e-3
NODES = 24
RANK = 8
PAD = 80
F32 = jnp.float32
BF16 = jnp.bfloat16
MIB = 1024 * 1024


def split_np(values):
    high = values.astype(np.float32).astype(ml_dtypes.bfloat16)
    low = (values - high.astype(np.float64)).astype(np.float32).astype(ml_dtypes.bfloat16)
    return high, low


def log_range():
    low, high = np.log(RATE_MIN + SHIFT), np.log(RATE_MAX + SHIFT)
    return (low + high) / 2, (high - low) / 2


def basis_of(count):
    rates = np.linspace(RATE_MIN, RATE_MAX, 1500)
    basis = np.linalg.svd(np.exp(-np.outer(rates, np.arange(count))), full_matrices=False)[2][:RANK]
    return basis * np.sign(basis[:, :1])


@functools.lru_cache(maxsize=None)
def tables(block, devices):
    mid, half = log_range()
    order = np.arange(NODES)
    node_x = np.cos((2 * order + 1) * np.pi / (2 * NODES))
    nodes = np.exp(mid + half * node_x) - SHIFT
    weights = np.full(NODES, 2.0 / NODES)
    weights[0] = 1.0 / NODES
    to_nodes = np.cos(order[None, :] * np.arccos(node_x)[:, None]) * weights[None, :]

    lags = np.arange(block)
    near, wide = basis_of(block), basis_of(2 * block)
    near_share = np.exp(-np.outer(nodes, lags)) @ near.T
    wide_share = np.exp(-np.outer(nodes, np.arange(2 * block))) @ wide.T
    mix = np.concatenate([to_nodes, near_share.T @ to_nodes], 0).astype(np.float32)

    lag = lags[:, None] - lags[None, :]
    toeplitz = np.where(lag >= 0, near[:, np.maximum(lag, 0)], 0.0).reshape(RANK * block, block)
    toeplitz = np.concatenate(split_np(toeplitz), 1)
    near_back, wide_back = near[:, ::-1], wide[:, ::-1]
    moment = np.concatenate([wide_back[:, :block], near_back, wide_back[:, block:], near_back], 0)
    moment = np.concatenate(split_np(moment), 1)
    first = np.zeros((2 * RANK, 128), np.float32)
    first[:RANK, 0:2] = wide_back[:, :2]
    first[:RANK, 2:4] = wide_back[:, block : block + 2]
    first[RANK:, 0:2] = near_back[:, :2]

    chips = devices // 2
    place = np.arange(devices)
    gap = (place // 2)[:, None] - 1 - np.arange(chips)[None, :]
    lead = (2 * np.maximum(gap, 0) + (place % 2)[:, None]) * block
    decay = np.where(gap[:, None, :] >= 0, np.exp(-nodes[None, :, None] * lead[:, None, :]), 0.0)
    carry = (decay[:, :, :, None] * wide_share[None, :, None, :]).reshape(devices, NODES, chips * RANK)
    carry = np.concatenate(split_np(carry), 1).reshape(devices * 2 * NODES, chips * RANK)

    parts = [np.exp(-np.outer(lags + 1 - by, nodes)) * (lags >= by - 1)[:, None] for by in (0, 1, 2)]
    spread = np.concatenate(parts + [np.zeros((block, PAD - 3 * NODES))], 1)
    high, low = split_np(spread)
    spread = np.concatenate([high, low, high], 1)
    return mix, toeplitz, moment, first, near_share.astype(np.float32), carry, spread


def split(values):
    high = values.astype(BF16)
    return high, (values - high.astype(F32)).astype(BF16)


def dot(left, right):
    return jnp.dot(left, right, preferred_element_type=F32)


def exact_dot(left, right):
    return jnp.dot(left, right, preferred_element_type=F32, precision=lax.Precision.HIGHEST)


def rounded(values):
    return values.astype(BF16).astype(F32)


def zeros(rows, columns):
    return jnp.zeros((rows, columns), F32)


def edge_kernel(q_ref, k_ref, v_ref, tails_ref, edges_ref, held, sems):
    block, columns = q_ref.shape
    copies = []
    for idx, (ref, start) in enumerate(
        ((q_ref, block - 16), (k_ref, block - 16), (v_ref, block - 16), (k_ref, 0), (v_ref, 0))
    ):
        copies.append(pltpu.make_async_copy(ref.at[pl.ds(start, 16)], held.at[idx], sems.at[idx]))
    for copy in copies:
        copy.start()
    for copy in copies:
        copy.wait()
    rows = [held[idx].astype(F32)[14:16] for idx in range(3)]
    rows += [held[idx].astype(F32)[0:2] for idx in (3, 4)]
    tails_ref[...] = jnp.concatenate(rows[:3] + [zeros(2, columns)], 0).astype(BF16)
    edges_ref[...] = jnp.concatenate(rows + [zeros(6, columns)], 0).astype(BF16)


def featurize(values, taps):
    return rounded(
        taps[0:1] * values + taps[1:2] * pltpu.roll(values, 1, 0) + taps[2:3] * pltpu.roll(values, 2, 0)
    )


def moment_kernel(order_ref, k_ref, v_ref, taps_hbm, moment_hbm, parts_ref, held, taps_ref, moment_ref, sems):
    block, columns = k_ref.shape
    width = held.shape[-1]
    steps = columns // width
    copies = []
    for step in range(steps):
        cols = pl.ds(step * width, width)
        copies.append(
            [
                pltpu.make_async_copy(ref.at[:, cols], held.at[idx, step], sems.at[2 * step + idx])
                for idx, ref in enumerate((k_ref, v_ref))
            ]
        )
    copies[0].append(pltpu.make_async_copy(taps_hbm, taps_ref, sems.at[2 * steps]))
    copies[0].append(pltpu.make_async_copy(moment_hbm, moment_ref, sems.at[2 * steps + 1]))
    for group in copies:
        for copy in group:
            copy.start()
    core = lax.rem(lax.axis_index("ctx"), 2)
    row = lax.broadcasted_iota(jnp.int32, (block, width), 0)
    for step in range(steps):
        cols = slice(step * width, (step + 1) * width)
        for copy in copies[step]:
            copy.wait()
        moment = moment_ref[pl.ds(pl.multiple_of(core * 2 * RANK, 2 * RANK), 2 * RANK)]
        key_feat = featurize(held[0, step].astype(F32), taps_ref[1, :, cols])
        value_feat = featurize(held[1, step].astype(F32), taps_ref[2, :, cols])
        product = jnp.where(row < 2, 0.0, key_feat * value_feat).astype(BF16)
        parts_ref[:, cols] = dot(moment, jnp.concatenate([product, product], 0))


def merge_kernel(mine_ref, other_ref, halo_ref, halo_other_ref, parts_ref, parts_other_ref, taps_ref, first_ref,
                 sent_ref, side_ref, held, sem):
    lower = lax.rem(lax.axis_index("ctx"), 2) == 0
    mine, other = mine_ref[...].astype(F32), other_ref[...].astype(F32)
    before = halo_ref[...].astype(F32) + halo_other_ref[...].astype(F32)
    edges0, edges1 = jnp.where(lower, mine, other), jnp.where(lower, other, mine)
    parts, parts_other = parts_ref[...], parts_other_ref[...]
    parts0, parts1 = jnp.where(lower, parts, parts_other), jnp.where(lower, parts_other, parts)

    def two_rows(head, tail, taps):
        row0 = taps[0:1] * head[0:1] + taps[1:2] * tail[1:2] + taps[2:3] * tail[0:1]
        row1 = taps[0:1] * head[1:2] + taps[1:2] * head[0:1] + taps[2:3] * tail[1:2]
        return rounded(row0), rounded(row1)

    def product_rows(edges, tails):
        key = two_rows(edges[6:8], tails[2:4], taps_ref[1])
        value = two_rows(edges[8:10], tails[4:6], taps_ref[2])
        return rounded(key[0] * value[0]), rounded(key[1] * value[1])

    a0, a1 = product_rows(edges0, before)
    b0, b1 = product_rows(edges1, edges0)
    first = first_ref[...]
    wide, close = first[:RANK], first[RANK:]
    near = parts0[RANK:] + close[:, 0:1] * a0 + close[:, 1:2] * a1
    columns = near.shape[1]
    held[...] = jnp.concatenate(
        [
            jnp.where(lower, a0, b0),
            jnp.where(lower, a1, b1),
            jnp.where(lower, before[0:2], edges0[0:2]),
            zeros(4, columns),
            jnp.where(lower, 0.0, near),
        ],
        0,
    )
    copy = pltpu.make_async_copy(held, side_ref, sem)
    copy.start()
    whole = parts0[:RANK] + parts1[:RANK]
    whole += wide[:, 0:1] * a0 + wide[:, 1:2] * a1 + wide[:, 2:3] * b0 + wide[:, 3:4] * b1
    pair = jnp.concatenate([whole, whole], 0).astype(BF16)
    for idx in range(sent_ref.shape[0] // 16):
        sent_ref[idx * 16 : idx * 16 + 16] = pair
    copy.wait()


def local_kernel(q_ref, k_ref, v_ref, side_ref, taps_ref, skip_ref, rates_ref, residues_ref, mix_ref, toeplitz_ref,
                 near_ref, spread_ref, feat_ref, full_ref, local_ref, weight_ref, cheb_ref):
    mid, half = log_range()
    x = (jnp.log(rates_ref[...] + SHIFT) - mid) * (1.0 / half)
    before = residues_ref[...]
    now = before * x
    cheb_ref[0:1] = jnp.sum(before, 0, keepdims=True)
    cheb_ref[1:2] = jnp.sum(now, 0, keepdims=True)
    twice = 2.0 * x
    for order in range(2, NODES):
        before, now = now, twice * now - before
        cheb_ref[order : order + 1] = jnp.sum(now, 0, keepdims=True)
    mixed = exact_dot(mix_ref[...], cheb_ref[...])
    weight = mixed[:NODES]

    side = side_ref[...]
    row0, row1, edge = side[0:1], side[1:2], side[2:4]
    columns = side.shape[1]
    weight_ref[...] = jnp.concatenate([weight, skip_ref[...], zeros(7, columns)], 0)
    stacked = jnp.concatenate(
        [weight * exact_dot(near_ref[...], side[8:]), weight * row0, weight * row1,
         zeros(PAD - 3 * NODES, columns)], 0
    )
    high, low = split(stacked)
    stacked = jnp.concatenate([high, high, low], 0)
    block = q_ref.shape[0]
    row = lax.broadcasted_iota(jnp.int32, (block, columns), 0)
    product = featurize(k_ref[...].astype(F32), taps_ref[1]) * featurize(v_ref[...].astype(F32), taps_ref[2])
    full_ref[...] = jnp.where(row == 0, row0, jnp.where(row == 1, row1, product)).astype(BF16)
    product = jnp.where(row < 2, 0.0, product).astype(BF16)
    twin = jnp.concatenate([product, product], 0)
    for half_idx in range(columns // 256):
        cols = slice(half_idx * 256, half_idx * 256 + 256)
        total = dot(spread_ref[...], stacked[:, cols])
        for k in range(RANK):
            total += mixed[NODES + k : NODES + k + 1, cols] * dot(
                toeplitz_ref[k * block : (k + 1) * block], twin[:, cols]
            )
        local_ref[:, cols] = total

    values = q_ref[...].astype(F32)
    taps = taps_ref[0]
    one = jnp.where(row == 0, edge[1:2], pltpu.roll(values, 1, 0))
    two = jnp.where(row == 0, edge[0:1], jnp.where(row == 1, edge[1:2], pltpu.roll(values, 2, 0)))
    feat_ref[...] = (taps[0:1] * values + taps[1:2] * one + taps[2:3] * two).astype(BF16)


def out_kernel(feat_ref, full_ref, local_ref, weight_ref, got_ref, carry_ref, spread_ref, out_ref, held, sems):
    place = lax.axis_index("ctx")
    carry = carry_ref[pl.ds(pl.multiple_of(place * 2 * NODES, 2 * NODES), 2 * NODES)]
    width = held.shape[-1]
    copies = []
    for step in range(held.shape[0]):
        cols = slice(step * width, (step + 1) * width)
        state = dot(carry, got_ref[:, cols])
        state = weight_ref[:NODES, cols] * (state[:NODES] + state[NODES:])
        high, low = split(jnp.concatenate([state, zeros(PAD - NODES, width)], 0))
        convolved = local_ref[:, cols] + dot(spread_ref[...], jnp.concatenate([high, high, low], 0))
        skip = weight_ref[NODES : NODES + 1, cols]
        held[step] = (
            feat_ref[:, cols].astype(F32) * (rounded(convolved) + skip * full_ref[:, cols].astype(F32))
        ).astype(BF16)
        copies.append(pltpu.make_async_copy(held.at[step], out_ref.at[:, pl.ds(step * width, width)], sems.at[step]))
        copies[-1].start()
    for copy in copies:
        copy.wait()


def on_device(query_proj, key_proj, value_proj, short_filter, skip_gain, pole_rates, pole_residues):
    block, channels = query_proj.shape
    devices = lax.axis_size("ctx")
    poles = pole_rates.shape[1]
    mix, toeplitz, moment, first, near, carry, spread = (jnp.asarray(table) for table in tables(block, devices))
    width = 512
    grid = (channels // width,)

    def cols(rows):
        return pl.BlockSpec((rows, width), lambda i: (0, i))

    def fixed(array):
        return pl.BlockSpec(array.shape, lambda i: (0,) * array.ndim)

    taps_spec = pl.BlockSpec((3, 3, width), lambda i: (0, 0, i))
    hbm = pl.BlockSpec(memory_space=pltpu.HBM)
    vmem = pl.BlockSpec(memory_space=pltpu.VMEM)
    params = pltpu.CompilerParams(vmem_limit_bytes=32 * MIB)
    keep = functools.partial(pltpu.with_memory_space_constraint, memory_space=pltpu.HBM)
    query_proj, key_proj, value_proj = keep(query_proj), keep(key_proj), keep(value_proj)
    swap = [(i, i ^ 1) for i in range(devices)]

    tails, edges = pl.pallas_call(
        edge_kernel,
        in_specs=[hbm, hbm, hbm],
        out_specs=[vmem, vmem],
        out_shape=[pltpu.VMEM((8, channels), BF16), pltpu.VMEM((16, channels), BF16)],
        scratch_shapes=[pltpu.VMEM((5, 16, channels), BF16), pltpu.SemaphoreType.DMA((5,))],
        compiler_params=params,
        name="edges",
    )(query_proj, key_proj, value_proj)
    halo = lax.ppermute(tails, "ctx", [(i, i + 1) for i in range(1, devices - 1, 2)])
    edges_other = lax.ppermute(edges, "ctx", swap)

    parts = pl.pallas_call(
        moment_kernel,
        in_specs=[pl.BlockSpec(memory_space=pl.ANY), hbm, hbm, hbm, hbm],
        out_specs=vmem,
        out_shape=pltpu.VMEM((2 * RANK, channels), F32),
        scratch_shapes=[
            pltpu.VMEM((2, channels // width, block, width), BF16),
            pltpu.VMEM(short_filter.shape, F32),
            pltpu.VMEM(moment.shape, BF16),
            pltpu.SemaphoreType.DMA((2 * (channels // width) + 2,)),
        ],
        compiler_params=params,
        cost_estimate=pl.CostEstimate(
            flops=1, bytes_accessed=1, transcendentals=0
        ),
        name="moments",
    )(edges, key_proj, value_proj, keep(short_filter), keep(moment))
    parts, halo = lax.optimization_barrier((parts, halo))
    parts_other = lax.ppermute(parts, "ctx", swap)
    halo_other = lax.ppermute(halo, "ctx", swap)

    sent, side = pl.pallas_call(
        merge_kernel,
        in_specs=[vmem] * 8,
        out_specs=[vmem, hbm],
        out_shape=[
            pltpu.VMEM((devices // 2 * RANK, channels), BF16),
            pltpu.HBM((2 * RANK, channels), F32),
        ],
        scratch_shapes=[pltpu.VMEM((2 * RANK, channels), F32), pltpu.SemaphoreType.DMA],
        compiler_params=params,
        name="merge",
    )(edges, edges_other, halo, halo_other, parts, parts_other, short_filter, first)

    groups = [list(range(core, devices, 2)) for core in range(2)]
    got = lax.all_to_all(sent, "ctx", 0, 0, axis_index_groups=groups, tiled=True)

    local_args = (query_proj, key_proj, value_proj, side, short_filter, skip_gain.reshape(1, -1), pole_rates.T,
                  pole_residues.T, mix, toeplitz, near, spread)
    feat, full, local, weight = pl.pallas_call(
        local_kernel,
        grid=grid,
        in_specs=[cols(block), cols(block), cols(block), cols(2 * RANK), taps_spec, cols(1), cols(poles), cols(poles),
                  fixed(mix), fixed(toeplitz), fixed(near), fixed(spread)],
        out_specs=[cols(block), cols(block), cols(block), cols(NODES + 8)],
        out_shape=[
            pltpu.VMEM((block, channels), BF16),
            pltpu.VMEM((block, channels), BF16),
            pltpu.VMEM((block, channels), F32),
            pltpu.VMEM((NODES + 8, channels), F32),
        ],
        scratch_shapes=[pltpu.VMEM((NODES, width), F32)],
        compiler_params=params,
        cost_estimate=pl.CostEstimate(
            flops=8 * toeplitz.size * channels, bytes_accessed=16 * block * channels, transcendentals=0
        ),
        name="local",
    )(*(keep(arg) for arg in local_args))

    return pl.pallas_call(
        out_kernel,
        in_specs=[vmem] * 7,
        out_specs=hbm,
        out_shape=pltpu.HBM((block, channels), BF16),
        scratch_shapes=[
            pltpu.VMEM((channels // width, block, width), BF16),
            pltpu.SemaphoreType.DMA((channels // width,)),
        ],
        compiler_params=params,
        name="output",
    )(feat, full, local, weight, got, carry, spread)


def solution(mesh):
    placed = (
        P("ctx", "tp"),
        P("ctx", "tp"),
        P("ctx", "tp"),
        P(None, None, "tp"),
        P("tp"),
        P("tp", None),
        P("tp", None),
    )
    return jax.shard_map(
        on_device, mesh=mesh, in_specs=placed, out_specs=P("ctx", "tp"), check_vma=False
    )
```

```python
import functools

import jax
import jax.numpy as jnp
import ml_dtypes
import numpy as np
from jax import lax
from jax.experimental import pallas as pl
from jax.experimental.pallas import tpu as pltpu
from jax.sharding import PartitionSpec as P

RATE_MIN, RATE_MAX = 0.3 / 4096, 1.0 / 30.0
SHIFT = 1.2e-3
NODES = 24
RANK = 8
PAD = 80
F32 = jnp.float32
BF16 = jnp.bfloat16
MIB = 1024 * 1024


def split_np(values):
    high = values.astype(np.float32).astype(ml_dtypes.bfloat16)
    low = (values - high.astype(np.float64)).astype(np.float32).astype(ml_dtypes.bfloat16)
    return high, low


def log_range():
    low, high = np.log(RATE_MIN + SHIFT), np.log(RATE_MAX + SHIFT)
    return (low + high) / 2, (high - low) / 2


def basis_of(count):
    rates = np.linspace(RATE_MIN, RATE_MAX, 1500)
    basis = np.linalg.svd(np.exp(-np.outer(rates, np.arange(count))), full_matrices=False)[2][:RANK]
    return basis * np.sign(basis[:, :1])


def chip_order(chips):
    return list(range(chips))[::-1]


@functools.lru_cache(maxsize=None)
def tables(block, devices):
    mid, half = log_range()
    order = np.arange(NODES)
    node_x = np.cos((2 * order + 1) * np.pi / (2 * NODES))
    nodes = np.exp(mid + half * node_x) - SHIFT
    weights = np.full(NODES, 2.0 / NODES)
    weights[0] = 1.0 / NODES
    to_nodes = np.cos(order[None, :] * np.arccos(node_x)[:, None]) * weights[None, :]

    lags = np.arange(block)
    near, wide = basis_of(block), basis_of(2 * block + 2)
    near_share = np.exp(-np.outer(nodes, lags)) @ near.T
    wide_share = np.exp(-np.outer(nodes, np.arange(2 * block + 2))) @ wide.T
    mix = np.concatenate([to_nodes, near_share.T @ to_nodes], 0).astype(np.float32)

    lag = lags[:, None] - lags[None, :]
    toeplitz = np.where(lag >= 0, near[:, np.maximum(lag, 0)], 0.0).reshape(RANK * block, block)
    toeplitz = np.concatenate(split_np(toeplitz), 1)
    near_back = near[:, ::-1]
    moment = np.concatenate(split_np(near_back), 1)
    first = np.zeros((2 * RANK, 128), np.float32)
    first[:RANK, 0:2] = near_back[:, :2]
    first[:RANK, 2:4] = near_back[:, -2:]
    first[RANK:, 0:2] = wide[:, 1::-1]
    widen = np.concatenate([wide[:, block + 2 :] @ near.T, wide[:, 2 : block + 2] @ near.T], 1)
    high, low = split_np(widen)
    widen = np.concatenate([high, low, high, np.zeros_like(high)], 1)

    chips = devices // 2
    place = np.arange(devices)
    gap = (place // 2)[:, None] - 1 - np.array(chip_order(chips))[None, :]
    lead = 2 * block * np.maximum(gap, 0) + (place % 2)[:, None] * (block - 2)
    decay = np.where(gap[:, None, :] >= 0, np.exp(-nodes[None, :, None] * lead[:, None, :]), 0.0)
    carry = (decay[:, :, :, None] * wide_share[None, :, None, :]).reshape(devices, NODES, chips * RANK)
    carry = np.concatenate(split_np(carry), 1).reshape(devices * 2 * NODES, chips * RANK)

    upper = [np.exp(-np.outer(lags + 1 - by, nodes)) * (lags >= by - 1)[:, None] for by in (0, 1, 2)]
    lower = [np.exp(-np.outer(lags - 1, nodes)), np.zeros((block, NODES)), -np.exp(nodes)[None, :] * (lags == 0)[:, None]]
    spread = []
    for parts in (lower, upper):
        high, low = split_np(np.concatenate(parts + [np.zeros((block, PAD - 3 * NODES))], 1))
        spread.append(np.concatenate([high, low, high], 1))
    spread = np.concatenate(spread, 0)
    high, low = split_np(near_share)
    near_share = np.concatenate([high, low, high, np.zeros_like(high)], 1)
    return mix, toeplitz, moment, first, widen, near_share, carry, spread


def split(values):
    high = values.astype(BF16)
    return high, (values - high.astype(F32)).astype(BF16)


def dot(left, right):
    return jnp.dot(left, right, preferred_element_type=F32)


def exact_dot(left, right):
    return jnp.dot(left, right, preferred_element_type=F32, precision=lax.Precision.HIGHEST)


def rounded(values):
    return values.astype(BF16).astype(F32)


def zeros(rows, columns):
    return jnp.zeros((rows, columns), F32)


def edge_kernel(q_ref, k_ref, v_ref, edges_ref, outer_ref, held, sems):
    block, columns = q_ref.shape
    copies = []
    for idx, (ref, start) in enumerate(
        ((q_ref, block - 16), (k_ref, block - 16), (v_ref, block - 16), (k_ref, 0), (v_ref, 0))
    ):
        copies.append(pltpu.make_async_copy(ref.at[pl.ds(start, 16)], held.at[idx], sems.at[idx]))
    for copy in copies:
        copy.start()
    for copy in copies:
        copy.wait()
    tails = [held[idx].astype(F32)[14:16] for idx in range(3)]
    heads = [held[idx].astype(F32)[0:2] for idx in (3, 4)]
    edges_ref[...] = jnp.concatenate(tails + heads + [zeros(6, columns)], 0).astype(BF16)
    lower = lax.rem(lax.axis_index("ctx"), 2) == 0
    outer = jnp.where(
        lower, jnp.concatenate(heads + [zeros(4, columns)], 0), jnp.concatenate(tails + [zeros(2, columns)], 0)
    )
    outer_ref[...] = outer.astype(BF16)


def featurize(values, taps):
    row = lax.broadcasted_iota(jnp.int32, values.shape, 0)
    one = jnp.where(row < 1, 0.0, pltpu.roll(values, 1, 0))
    two = jnp.where(row < 2, 0.0, pltpu.roll(values, 2, 0))
    return rounded(taps[0:1] * values + taps[1:2] * one + taps[2:3] * two)


def moment_kernel(edges_ref, k_ref, v_ref, taps_hbm, moment_hbm, near_ref, inner_ref, held, taps_ref, moment_ref,
                  sems):
    block, columns = k_ref.shape
    width = held.shape[-1]
    steps = columns // width
    copies = []
    for step in range(steps):
        cols = pl.ds(step * width, width)
        copies.append(
            [
                pltpu.make_async_copy(ref.at[:, cols], held.at[idx, step], sems.at[2 * step + idx])
                for idx, ref in enumerate((k_ref, v_ref))
            ]
        )
    copies[0].append(pltpu.make_async_copy(taps_hbm, taps_ref, sems.at[2 * steps]))
    copies[0].append(pltpu.make_async_copy(moment_hbm, moment_ref, sems.at[2 * steps + 1]))
    for group in copies:
        for copy in group:
            copy.start()
    row = lax.broadcasted_iota(jnp.int32, (block, width), 0)
    place = lax.axis_index("ctx")
    lower = lax.rem(place, 2) == 0
    first_row = jnp.where(place == 0, 0, 2)
    for step in range(steps):
        cols = slice(step * width, (step + 1) * width)
        for copy in copies[step]:
            copy.wait()
        key_feat = featurize(held[0, step].astype(F32), taps_ref[1, :, cols])
        value_feat = featurize(held[1, step].astype(F32), taps_ref[2, :, cols])
        product = jnp.where(row < first_row, 0.0, key_feat * value_feat).astype(BF16)
        near = dot(moment_ref[...], jnp.concatenate([product, product], 0))
        near_ref[:, cols] = near
        edges = edges_ref[:, cols].astype(F32)
        for_upper = jnp.concatenate([edges[0:6], zeros(2, width)], 0)
        for_lower = jnp.concatenate([edges[6:10], edges[2:6]], 0)
        inner_ref[:, cols] = jnp.concatenate([near, jnp.where(lower, for_upper, for_lower)], 0).astype(BF16)


def two_rows(head, tail, taps):
    row0 = taps[0:1] * head[0:1] + taps[1:2] * tail[1:2] + taps[2:3] * tail[0:1]
    row1 = taps[0:1] * head[1:2] + taps[1:2] * head[0:1] + taps[2:3] * tail[1:2]
    return rounded(row0), rounded(row1)


def product_rows(heads, tails, taps_ref):
    key = two_rows(heads[0:2], tails[0:2], taps_ref[1])
    value = two_rows(heads[2:4], tails[2:4], taps_ref[2])
    return rounded(key[0] * value[0]), rounded(key[1] * value[1])


def merge_kernel(edges_ref, inner_ref, outer_ref, outer_more_ref, near_ref, taps_ref, first_ref, widen_ref, sent_ref,
                 side_ref, held, sems):
    place = lax.axis_index("ctx")
    lower = lax.rem(place, 2) == 0
    edges, inner = edges_ref[...].astype(F32), inner_ref[...].astype(F32)
    outer, outer_more = outer_ref[...].astype(F32), outer_more_ref[...].astype(F32)
    a0, a1 = product_rows(edges[6:10], outer[2:6], taps_ref)
    b0, b1 = product_rows(
        jnp.where(lower, inner[8:12], edges[6:10]), jnp.where(lower, edges[2:6], inner[10:14]), taps_ref
    )
    c0, c1 = product_rows(
        jnp.where(lower, outer_more[0:4], outer[0:4]), jnp.where(lower, inner[12:16], edges[2:6]), taps_ref
    )
    near, near_other = near_ref[...], inner[:RANK]
    first, last = first_ref[:RANK], first_ref[RANK:]
    near0 = jnp.where(lower, near, near_other)
    near1 = jnp.where(lower, near_other, near) + first[:, 0:1] * b0 + first[:, 1:2] * b1
    high, low = split(jnp.concatenate([near0, near1], 0))
    whole = dot(widen_ref[...], jnp.concatenate([high, high, low, jnp.zeros_like(low)], 0))
    whole += last[:, 0:1] * c0 + last[:, 1:2] * c1
    held[...] = jnp.concatenate([whole, whole], 0).astype(BF16)
    copies = [
        pltpu.make_async_copy(held, sent_ref.at[pl.ds(idx * 16, 16)], sems.at[idx])
        for idx in range(sent_ref.shape[0] // 16)
    ]
    for copy in copies:
        copy.start()
    start = jnp.where(place == 0, first[:, 2:3] * a0 + first[:, 3:4] * a1, 0.0)
    side_ref[...] = jnp.concatenate(
        [
            jnp.where(lower, a0, b0),
            jnp.where(lower, a1, b1),
            jnp.where(lower, outer[0:2], inner[8:10]),
            zeros(4, a0.shape[1]),
            jnp.where(lower, start, near0),
        ],
        0,
    )
    for copy in copies:
        copy.wait()


def local_kernel(side_ref, q_hbm, k_hbm, v_hbm, taps_hbm, skip_hbm, rates_hbm, residues_hbm, mix_hbm, toeplitz_hbm,
                 near_hbm, spread_hbm, feat_ref, full_ref, local_ref, weight_ref, q_ref, k_ref, v_ref, taps_ref,
                 skip_ref, rates_ref, residues_ref, mix_ref, toeplitz_ref, near_ref, spread_ref, cheb_ref, sems):
    block, channels = q_ref.shape
    width = cheb_ref.shape[1]
    steps = channels // width
    count = 0

    def load(source, target):
        nonlocal count
        copy = pltpu.make_async_copy(source, target, sems.at[count])
        copy.start()
        count += 1
        return copy

    filters = [load(rates_hbm, rates_ref), load(residues_hbm, residues_ref), load(mix_hbm, mix_ref),
               load(skip_hbm, skip_ref)]
    rows = [load(taps_hbm, taps_ref), load(near_hbm, near_ref)]
    signals = []
    for step in range(steps):
        at = (slice(None), pl.ds(step * width, width))
        signals.append([load(k_hbm.at[at], k_ref.at[at]), load(v_hbm.at[at], v_ref.at[at])])
        if step == 0:
            matrices = [load(spread_hbm, spread_ref), load(toeplitz_hbm, toeplitz_ref)]
    queries = []
    for step in range(steps):
        at = (slice(None), pl.ds(step * width, width))
        queries.append(load(q_hbm.at[at], q_ref.at[at]))

    mid, half = log_range()
    core = lax.rem(lax.axis_index("ctx"), 2)
    row = lax.broadcasted_iota(jnp.int32, (block, width), 0)
    for copy in filters:
        copy.wait()
    for step in range(steps):
        cols = slice(step * width, (step + 1) * width)
        x = (jnp.log(rates_ref[:, cols] + SHIFT) - mid) * (1.0 / half)
        before = residues_ref[:, cols]
        now = before * x
        cheb_ref[0:1] = jnp.sum(before, 0, keepdims=True)
        cheb_ref[1:2] = jnp.sum(now, 0, keepdims=True)
        twice = 2.0 * x
        for order in range(2, NODES):
            before, now = now, twice * now - before
            cheb_ref[order : order + 1] = jnp.sum(now, 0, keepdims=True)
        mixed = exact_dot(mix_ref[...], cheb_ref[...])
        weight = mixed[:NODES]
        weight_ref[:, cols] = jnp.concatenate([weight, skip_ref[:, cols], zeros(7, width)], 0)

        if step == 0:
            for copy in rows:
                copy.wait()
        side = side_ref[:, cols]
        row0, row1, edge, moment = side[0:1], side[1:2], side[2:4], side[8:]
        high, low = split(moment)
        state = dot(near_ref[...], jnp.concatenate([high, high, low, jnp.zeros_like(low)], 0))
        stacked = jnp.concatenate(
            [weight * state, weight * row0, weight * row1, zeros(PAD - 3 * NODES, width)], 0
        )
        high, low = split(stacked)
        stacked = jnp.concatenate([high, high, low], 0)

        for copy in signals[step]:
            copy.wait()
        product = featurize(k_ref[:, cols].astype(F32), taps_ref[1, :, cols]) * featurize(
            v_ref[:, cols].astype(F32), taps_ref[2, :, cols]
        )
        full_ref[:, cols] = jnp.where(row == 0, row0, jnp.where(row == 1, row1, product)).astype(BF16)
        product = jnp.where(row < 2, 0.0, product).astype(BF16)
        twin = jnp.concatenate([product, product], 0)
        if step == 0:
            for copy in matrices:
                copy.wait()
        for part in range(width // 256):
            inner = slice(part * 256, part * 256 + 256)
            total = dot(spread_ref[pl.ds(pl.multiple_of(core * block, block), block)], stacked[:, inner])
            for k in range(RANK):
                total += mixed[NODES + k : NODES + k + 1, inner] * dot(
                    toeplitz_ref[k * block : (k + 1) * block], twin[:, inner]
                )
            local_ref[:, step * width + part * 256 : step * width + part * 256 + 256] = total

        queries[step].wait()
        values = q_ref[:, cols].astype(F32)
        taps = taps_ref[0, :, cols]
        one = jnp.where(row == 0, edge[1:2], pltpu.roll(values, 1, 0))
        two = jnp.where(row == 0, edge[0:1], jnp.where(row == 1, edge[1:2], pltpu.roll(values, 2, 0)))
        feat_ref[:, cols] = (taps[0:1] * values + taps[1:2] * one + taps[2:3] * two).astype(BF16)


def out_kernel(feat_ref, full_ref, local_ref, weight_ref, got_ref, carry_ref, spread_ref, out_ref, held, sems):
    place = lax.axis_index("ctx")
    carry = carry_ref[pl.ds(pl.multiple_of(place * 2 * NODES, 2 * NODES), 2 * NODES)]
    _, block, width = held.shape
    spread = spread_ref[pl.ds(pl.multiple_of(lax.rem(place, 2) * block, block), block)]
    copies = []
    for step in range(held.shape[0]):
        cols = slice(step * width, (step + 1) * width)
        state = dot(carry, got_ref[:, cols])
        state = weight_ref[:NODES, cols] * (state[:NODES] + state[NODES:])
        high, low = split(jnp.concatenate([state, zeros(PAD - NODES, width)], 0))
        convolved = local_ref[:, cols] + dot(spread, jnp.concatenate([high, high, low], 0))
        skip = weight_ref[NODES : NODES + 1, cols]
        held[step] = (
            feat_ref[:, cols].astype(F32) * (rounded(convolved) + skip * full_ref[:, cols].astype(F32))
        ).astype(BF16)
        copies.append(pltpu.make_async_copy(held.at[step], out_ref.at[:, pl.ds(step * width, width)], sems.at[step]))
        copies[-1].start()
    for copy in copies:
        copy.wait()


def on_device(query_proj, key_proj, value_proj, short_filter, skip_gain, pole_rates, pole_residues):
    block, channels = query_proj.shape
    devices = lax.axis_size("ctx")
    poles = pole_rates.shape[1]
    mix, toeplitz, moment, first, widen, near, carry, spread = (jnp.asarray(table) for table in tables(block, devices))
    width = 512
    grid = (channels // width,)

    def cols(rows):
        return pl.BlockSpec((rows, width), lambda i: (0, i))

    def fixed(array):
        return pl.BlockSpec(array.shape, lambda i: (0,) * array.ndim)

    taps_spec = pl.BlockSpec((3, 3, width), lambda i: (0, 0, i))
    hbm = pl.BlockSpec(memory_space=pltpu.HBM)
    vmem = pl.BlockSpec(memory_space=pltpu.VMEM)
    params = pltpu.CompilerParams(vmem_limit_bytes=32 * MIB)
    keep = functools.partial(pltpu.with_memory_space_constraint, memory_space=pltpu.HBM)
    query_proj, key_proj, value_proj = keep(query_proj), keep(key_proj), keep(value_proj)
    swap = [(i, i ^ 1) for i in range(devices)]

    edges, outer = pl.pallas_call(
        edge_kernel,
        in_specs=[hbm, hbm, hbm],
        out_specs=[vmem, vmem],
        out_shape=[pltpu.VMEM((16, channels), BF16), pltpu.VMEM((8, channels), BF16)],
        scratch_shapes=[pltpu.VMEM((5, 16, channels), BF16), pltpu.SemaphoreType.DMA((5,))],
        compiler_params=params,
        name="edges",
    )(query_proj, key_proj, value_proj)
    between = [(i, i + 1) for i in range(1, devices - 1, 2)]
    outer = lax.ppermute(outer, "ctx", between + [(j, i) for i, j in between])

    near_sums, inner = pl.pallas_call(
        moment_kernel,
        in_specs=[vmem, hbm, hbm, hbm, hbm],
        out_specs=[vmem, vmem],
        out_shape=[pltpu.VMEM((RANK, channels), F32), pltpu.VMEM((2 * RANK, channels), BF16)],
        scratch_shapes=[
            pltpu.VMEM((2, channels // width, block, width), BF16),
            pltpu.VMEM(short_filter.shape, F32),
            pltpu.VMEM(moment.shape, BF16),
            pltpu.SemaphoreType.DMA((2 * (channels // width) + 2,)),
        ],
        compiler_params=params,
        cost_estimate=pl.CostEstimate(
            flops=1, bytes_accessed=1, transcendentals=0
        ),
        name="moments",
    )(edges, key_proj, value_proj, keep(short_filter), keep(moment))
    inner, outer = lax.optimization_barrier((inner, outer))
    inner = lax.ppermute(inner, "ctx", swap)
    outer_more = lax.ppermute(outer, "ctx", swap)

    sent, side = pl.pallas_call(
        merge_kernel,
        in_specs=[vmem] * 8,
        out_specs=[hbm, vmem],
        out_shape=[
            pltpu.HBM((devices // 2 * RANK, channels), BF16),
            pltpu.VMEM((2 * RANK, channels), F32),
        ],
        scratch_shapes=[pltpu.VMEM((16, channels), BF16), pltpu.SemaphoreType.DMA((devices // 2 * RANK // 16,))],
        compiler_params=params,
        name="merge",
    )(edges, inner, outer, outer_more, near_sums, short_filter, first, widen)

    groups = [[2 * chip + core for chip in chip_order(devices // 2)] for core in range(2)]
    got = lax.all_to_all(sent, "ctx", 0, 0, axis_index_groups=groups, tiled=True)

    local_args = tuple(
        keep(arg)
        for arg in (query_proj, key_proj, value_proj, short_filter, skip_gain.reshape(1, -1), pole_rates.T,
                    pole_residues.T, mix, toeplitz, near, spread)
    )
    feat, full, local, weight = pl.pallas_call(
        local_kernel,
        in_specs=[vmem] + [hbm] * len(local_args),
        out_specs=[vmem] * 4,
        out_shape=[
            pltpu.VMEM((block, channels), BF16),
            pltpu.VMEM((block, channels), BF16),
            pltpu.VMEM((block, channels), F32),
            pltpu.VMEM((NODES + 8, channels), F32),
        ],
        scratch_shapes=[pltpu.VMEM(arg.shape, arg.dtype) for arg in local_args]
        + [pltpu.VMEM((NODES, width), F32), pltpu.SemaphoreType.DMA((9 + 3 * (channels // width),))],
        compiler_params=params,
        cost_estimate=pl.CostEstimate(
            flops=8 * toeplitz.size * channels, bytes_accessed=16 * block * channels, transcendentals=0
        ),
        name="local",
    )(side, *local_args)

    return pl.pallas_call(
        out_kernel,
        in_specs=[vmem] * 7,
        out_specs=hbm,
        out_shape=pltpu.HBM((block, channels), BF16),
        scratch_shapes=[
            pltpu.VMEM((channels // width, block, width), BF16),
            pltpu.SemaphoreType.DMA((channels // width,)),
        ],
        compiler_params=params,
        name="output",
    )(feat, full, local, weight, got, carry, spread)


def solution(mesh):
    placed = (
        P("ctx", "tp"),
        P("ctx", "tp"),
        P("ctx", "tp"),
        P(None, None, "tp"),
        P("tp"),
        P("tp", None),
        P("tp", None),
    )
    return jax.shard_map(
        on_device, mesh=mesh, in_specs=placed, out_specs=P("ctx", "tp"), check_vma=False
    )
```

```python
import functools

import jax
import jax.numpy as jnp
import ml_dtypes
import numpy as np
from jax import lax
from jax.experimental import pallas as pl
from jax.experimental.pallas import tpu as pltpu
from jax.sharding import PartitionSpec as P

RATE_MIN, RATE_MAX = 0.3 / 4096, 1.0 / 30.0
SHIFT = 1.2e-3
NODES = 24
RANK = 8
PAD = 80
ROW = 4
F32 = jnp.float32
BF16 = jnp.bfloat16
MIB = 1024 * 1024


def split_np(values):
    high = values.astype(np.float32).astype(ml_dtypes.bfloat16)
    low = (values - high.astype(np.float64)).astype(np.float32).astype(ml_dtypes.bfloat16)
    return high, low


def log_range():
    low, high = np.log(RATE_MIN + SHIFT), np.log(RATE_MAX + SHIFT)
    return (low + high) / 2, (high - low) / 2


def basis_of(count):
    rates = np.linspace(RATE_MIN, RATE_MAX, 1500)
    basis = np.linalg.svd(np.exp(-np.outer(rates, np.arange(count))), full_matrices=False)[2][:RANK]
    return basis * np.sign(basis[:, :1])


def shift_of(chip):
    return 0 if chip % ROW == 0 else 2


ORDER = (10, 14, 11, 15, 6, 7, 13, 9, 3, 2, 5, 8, 12, 1, 4, 0)


def chip_order(chips):
    return ORDER if chips == len(ORDER) else tuple(range(chips))


@functools.lru_cache(maxsize=None)
def tables(block, devices):
    mid, half = log_range()
    order = np.arange(NODES)
    node_x = np.cos((2 * order + 1) * np.pi / (2 * NODES))
    nodes = np.exp(mid + half * node_x) - SHIFT
    weights = np.full(NODES, 2.0 / NODES)
    weights[0] = 1.0 / NODES
    to_nodes = np.cos(order[None, :] * np.arccos(node_x)[:, None]) * weights[None, :]

    lags = np.arange(block)
    near, wide = basis_of(block), basis_of(2 * block + 2)
    near_share = np.exp(-np.outer(nodes, lags)) @ near.T
    wide_share = np.exp(-np.outer(nodes, np.arange(2 * block + 2))) @ wide.T
    mix = np.concatenate([to_nodes, near_share.T @ to_nodes], 0).astype(np.float32)

    lag = lags[:, None] - lags[None, :]
    toeplitz = np.where(lag >= 0, near[:, np.maximum(lag, 0)], 0.0).reshape(RANK * block, block)
    toeplitz = np.concatenate(split_np(toeplitz), 1)
    near_back = near[:, ::-1]
    moment = np.concatenate(split_np(near_back), 1)
    first = np.zeros((2 * RANK, 128), np.float32)
    first[:RANK, 0:2] = near_back[:, :2]
    first[RANK:, 0:2] = wide[:, 1::-1]
    widen = [
        np.concatenate([wide[:, by + block : by + 2 * block] @ near.T, wide[:, by : by + block] @ near.T], 1)
        for by in (0, 2)
    ]
    blank = np.zeros_like(widen[0])
    high, low = split_np(np.concatenate([widen[0], blank, widen[1], blank], 0))
    widen = np.concatenate([high, low, high, np.zeros_like(high)], 1)

    chips = devices // 2
    place = np.arange(devices)
    sources = np.array(chip_order(chips))
    starts = np.array([2 * block * (i // 2) + (block if i % 2 else shift_of(i // 2)) for i in place])
    ends = np.array([2 * block * (chip + 1) + shift_of(chip + 1) for chip in sources])
    lead = np.maximum(starts[:, None] - ends[None, :], 0)
    before = (place // 2)[:, None] > sources[None, :]
    decay = np.where(before[:, None, :], np.exp(-nodes[None, :, None] * lead[:, None, :]), 0.0)
    carry = (decay[:, :, :, None] * wide_share[None, :, None, :]).reshape(devices, NODES, chips * RANK)
    carry = np.concatenate(split_np(carry), 1).reshape(devices * 2 * NODES, chips * RANK)

    upper = [np.exp(-np.outer(lags + 1 - by, nodes)) * (lags >= by - 1)[:, None] for by in (0, 1, 2)]
    lower = [np.exp(-np.outer(lags - 1, nodes)), np.zeros((block, NODES)), -np.exp(nodes)[None, :] * (lags == 0)[:, None]]
    spread = []
    for parts in (lower, upper):
        high, low = split_np(np.concatenate(parts + [np.zeros((block, PAD - 3 * NODES))], 1))
        spread.append(np.concatenate([high, low, high], 1))
    spread = np.concatenate(spread, 0)
    high, low = split_np(near_share)
    near_share = np.concatenate([high, low, high, np.zeros_like(high)], 1)
    return mix, toeplitz, moment, first, widen, near_share, carry, spread


def split(values):
    high = values.astype(BF16)
    return high, (values - high.astype(F32)).astype(BF16)


def dot(left, right):
    return jnp.dot(left, right, preferred_element_type=F32)


def exact_dot(left, right):
    return jnp.dot(left, right, preferred_element_type=F32, precision=lax.Precision.HIGHEST)


def rounded(values):
    return values.astype(BF16).astype(F32)


def zeros(rows, columns):
    return jnp.zeros((rows, columns), F32)


def edge_kernel(q_ref, k_ref, v_ref, heads_ref, tails_ref, outer_ref, held, sems):
    block, columns = q_ref.shape
    copies = []
    for idx, ref in enumerate((k_ref, v_ref, q_ref)):
        copies.append(pltpu.make_async_copy(ref.at[pl.ds(0, 16)], held.at[idx], sems.at[idx]))
        copies.append(pltpu.make_async_copy(ref.at[pl.ds(block - 16, 16)], held.at[idx + 3], sems.at[idx + 3]))
    for copy in copies:
        copy.start()
    for copy in copies:
        copy.wait()
    heads = [held[idx].astype(F32)[0:2] for idx in range(3)]
    tails = [held[idx + 3].astype(F32)[14:16] for idx in range(3)]
    heads = jnp.concatenate(heads + [zeros(2, columns)], 0)
    tails = jnp.concatenate(tails + [zeros(2, columns)], 0)
    heads_ref[...] = heads.astype(BF16)
    tails_ref[...] = tails.astype(BF16)
    outer_ref[...] = jnp.where(lax.rem(lax.axis_index("ctx"), 2) == 0, heads, tails).astype(BF16)


def featurize(values, taps):
    row = lax.broadcasted_iota(jnp.int32, values.shape, 0)
    one = jnp.where(row < 1, 0.0, pltpu.roll(values, 1, 0))
    two = jnp.where(row < 2, 0.0, pltpu.roll(values, 2, 0))
    return rounded(taps[0:1] * values + taps[1:2] * one + taps[2:3] * two)


def moment_kernel(heads_ref, tails_ref, k_ref, v_ref, taps_ref, moment_ref, near_ref, inner_ref, *, width):
    block, columns = k_ref.shape
    steps = columns // width
    row = lax.broadcasted_iota(jnp.int32, (block, width), 0)
    for step in range(steps):
        cols = slice(step * width, (step + 1) * width)
        key_feat = featurize(k_ref[:, cols].astype(F32), taps_ref[1, :, cols])
        value_feat = featurize(v_ref[:, cols].astype(F32), taps_ref[2, :, cols])
        product = jnp.where(row < 2, 0.0, key_feat * value_feat).astype(BF16)
        near = dot(moment_ref[...], jnp.concatenate([product, product], 0))
        near_ref[:, cols] = near
        rows = [tails_ref[:, cols].astype(F32), heads_ref[:, cols].astype(F32), zeros(8, width)]
        inner_ref[:, cols] = jnp.concatenate([near] + rows, 0).astype(BF16)


def two_rows(head, tail, taps):
    row0 = taps[0:1] * head[0:1] + taps[1:2] * tail[1:2] + taps[2:3] * tail[0:1]
    row1 = taps[0:1] * head[1:2] + taps[1:2] * head[0:1] + taps[2:3] * tail[1:2]
    return rounded(row0), rounded(row1)


def product_rows(heads, tails, taps_ref):
    key = two_rows(heads[0:2], tails[0:2], taps_ref[1])
    value = two_rows(heads[2:4], tails[2:4], taps_ref[2])
    return rounded(key[0] * value[0]), rounded(key[1] * value[1])


def merge_kernel(heads_ref, tails_ref, inner_ref, outer_ref, outer_more_ref, near_ref, taps_ref, first_ref, widen_ref,
                 sent_ref, side_ref, held, sems):
    place = lax.axis_index("ctx")
    lower = lax.rem(place, 2) == 0
    chip = lax.div(place, 2)
    opens, closes = lax.rem(chip, ROW) == 0, lax.rem(chip + 1, ROW) == 0
    heads, tails, inner = heads_ref[...].astype(F32)[0:4], tails_ref[...].astype(F32)[0:4], inner_ref[...].astype(F32)
    outer, outer_more = outer_ref[...].astype(F32), outer_more_ref[...].astype(F32)
    tails_other, heads_other = inner[8:12], inner[16:20]
    heads0, heads1 = jnp.where(lower, heads, heads_other), jnp.where(lower, heads_other, heads)
    tails0, tails1 = jnp.where(lower, tails, tails_other), jnp.where(lower, tails_other, tails)
    outer0, outer1 = jnp.where(lower, outer, outer_more), jnp.where(lower, outer_more, outer)
    a0, a1 = product_rows(heads0, outer0[0:4], taps_ref)
    b0, b1 = product_rows(heads1, tails0, taps_ref)
    c0, c1 = (jnp.where(closes, 0.0, row) for row in product_rows(outer1[0:4], tails1, taps_ref))
    near, near_other = near_ref[...], inner[:RANK]
    first, last = first_ref[:RANK], first_ref[RANK:]
    near0 = jnp.where(lower, near, near_other)
    near0 += jnp.where(opens, first[:, 0:1] * a0 + first[:, 1:2] * a1, 0.0)
    near1 = jnp.where(lower, near_other, near) + first[:, 0:1] * b0 + first[:, 1:2] * b1
    high, low = split(jnp.concatenate([near0, near1], 0))
    widen = widen_ref[pl.ds(pl.multiple_of(jnp.where(closes, 0, 2 * RANK), 2 * RANK), 2 * RANK)]
    whole = dot(widen, jnp.concatenate([high, high, low, jnp.zeros_like(low)], 0))[:RANK]
    whole += last[:, 0:1] * c0 + last[:, 1:2] * c1
    held[...] = jnp.concatenate([whole, whole], 0).astype(BF16)
    copies = [
        pltpu.make_async_copy(held, sent_ref.at[pl.ds(idx * 16, 16)], sems.at[idx])
        for idx in range(sent_ref.shape[0] // 16)
    ]
    for copy in copies:
        copy.start()
    rows = [jnp.where(lower, a0, b0), jnp.where(lower, a1, b1), jnp.where(lower, outer[4:6], inner[12:14])]
    rows += [zeros(4, a0.shape[1]), jnp.where(lower, 0.0, near0)]
    side_ref[...] = jnp.concatenate(rows, 0)
    for copy in copies:
        copy.wait()


def spread_start(block):
    place = lax.axis_index("ctx")
    plain = jnp.logical_or(lax.rem(place, 2) == 1, lax.rem(lax.div(place, 2), ROW) == 0)
    return pl.multiple_of(jnp.where(plain, block, 0), block)


def local_kernel(side_ref, q_hbm, k_hbm, v_hbm, taps_hbm, skip_hbm, rates_hbm, residues_hbm, mix_hbm, toeplitz_hbm,
                 near_hbm, spread_hbm, feat_ref, full_ref, local_ref, weight_ref, q_ref, k_ref, v_ref, taps_ref,
                 skip_ref, rates_ref, residues_ref, mix_ref, toeplitz_ref, near_ref, spread_ref, cheb_ref, sems):
    block, channels = q_ref.shape
    width = cheb_ref.shape[1]
    steps = channels // width
    count = 0

    def load(source, target):
        nonlocal count
        copy = pltpu.make_async_copy(source, target, sems.at[count])
        copy.start()
        count += 1
        return copy

    filters = [load(rates_hbm, rates_ref), load(residues_hbm, residues_ref), load(mix_hbm, mix_ref),
               load(skip_hbm, skip_ref)]
    rows = [load(taps_hbm, taps_ref), load(near_hbm, near_ref)]
    signals = []
    for step in range(steps):
        at = (slice(None), pl.ds(step * width, width))
        signals.append([load(k_hbm.at[at], k_ref.at[at]), load(v_hbm.at[at], v_ref.at[at])])
        if step == 0:
            matrices = [load(spread_hbm, spread_ref), load(toeplitz_hbm, toeplitz_ref)]
    queries = []
    for step in range(steps):
        at = (slice(None), pl.ds(step * width, width))
        queries.append(load(q_hbm.at[at], q_ref.at[at]))

    mid, half = log_range()
    kind = spread_start(block)
    row = lax.broadcasted_iota(jnp.int32, (block, width), 0)
    for copy in filters:
        copy.wait()
    for step in range(steps):
        cols = slice(step * width, (step + 1) * width)
        x = (jnp.log(rates_ref[:, cols] + SHIFT) - mid) * (1.0 / half)
        before = residues_ref[:, cols]
        now = before * x
        cheb_ref[0:1] = jnp.sum(before, 0, keepdims=True)
        cheb_ref[1:2] = jnp.sum(now, 0, keepdims=True)
        twice = 2.0 * x
        for order in range(2, NODES):
            before, now = now, twice * now - before
            cheb_ref[order : order + 1] = jnp.sum(now, 0, keepdims=True)
        mixed = exact_dot(mix_ref[...], cheb_ref[...])
        weight = mixed[:NODES]
        weight_ref[:, cols] = jnp.concatenate([weight, skip_ref[:, cols], zeros(7, width)], 0)

        if step == 0:
            for copy in rows:
                copy.wait()
        side = side_ref[:, cols]
        row0, row1, edge, moment = side[0:1], side[1:2], side[2:4], side[8:]
        high, low = split(moment)
        state = dot(near_ref[...], jnp.concatenate([high, high, low, jnp.zeros_like(low)], 0))
        stacked = jnp.concatenate(
            [weight * state, weight * row0, weight * row1, zeros(PAD - 3 * NODES, width)], 0
        )
        high, low = split(stacked)
        stacked = jnp.concatenate([high, high, low], 0)

        for copy in signals[step]:
            copy.wait()
        product = featurize(k_ref[:, cols].astype(F32), taps_ref[1, :, cols]) * featurize(
            v_ref[:, cols].astype(F32), taps_ref[2, :, cols]
        )
        full_ref[:, cols] = jnp.where(row == 0, row0, jnp.where(row == 1, row1, product)).astype(BF16)
        product = jnp.where(row < 2, 0.0, product).astype(BF16)
        twin = jnp.concatenate([product, product], 0)
        if step == 0:
            for copy in matrices:
                copy.wait()
        for part in range(width // 256):
            inner = slice(part * 256, part * 256 + 256)
            total = dot(spread_ref[pl.ds(kind, block)], stacked[:, inner])
            for k in range(RANK):
                total += mixed[NODES + k : NODES + k + 1, inner] * dot(
                    toeplitz_ref[k * block : (k + 1) * block], twin[:, inner]
                )
            local_ref[:, step * width + part * 256 : step * width + part * 256 + 256] = total

        queries[step].wait()
        values = q_ref[:, cols].astype(F32)
        taps = taps_ref[0, :, cols]
        one = jnp.where(row == 0, edge[1:2], pltpu.roll(values, 1, 0))
        two = jnp.where(row == 0, edge[0:1], jnp.where(row == 1, edge[1:2], pltpu.roll(values, 2, 0)))
        feat_ref[:, cols] = (taps[0:1] * values + taps[1:2] * one + taps[2:3] * two).astype(BF16)


def out_kernel(feat_ref, full_ref, local_ref, weight_ref, got_ref, carry_ref, spread_ref, out_ref, held, sems):
    place = lax.axis_index("ctx")
    carry = carry_ref[pl.ds(pl.multiple_of(place * 2 * NODES, 2 * NODES), 2 * NODES)]
    _, block, width = held.shape
    spread = spread_ref[pl.ds(spread_start(block), block)]
    copies = []
    for step in range(held.shape[0]):
        cols = slice(step * width, (step + 1) * width)
        state = dot(carry, got_ref[:, cols])
        state = weight_ref[:NODES, cols] * (state[:NODES] + state[NODES:])
        high, low = split(jnp.concatenate([state, zeros(PAD - NODES, width)], 0))
        convolved = local_ref[:, cols] + dot(spread, jnp.concatenate([high, high, low], 0))
        skip = weight_ref[NODES : NODES + 1, cols]
        held[step] = (
            feat_ref[:, cols].astype(F32) * (rounded(convolved) + skip * full_ref[:, cols].astype(F32))
        ).astype(BF16)
        copies.append(pltpu.make_async_copy(held.at[step], out_ref.at[:, pl.ds(step * width, width)], sems.at[step]))
        copies[-1].start()
    for copy in copies:
        copy.wait()


def on_device(query_proj, key_proj, value_proj, short_filter, skip_gain, pole_rates, pole_residues):
    block, channels = query_proj.shape
    devices = lax.axis_size("ctx")
    poles = pole_rates.shape[1]
    mix, toeplitz, moment, first, widen, near, carry, spread = (jnp.asarray(table) for table in tables(block, devices))
    width = 512
    grid = (channels // width,)

    def cols(rows):
        return pl.BlockSpec((rows, width), lambda i: (0, i))

    def fixed(array):
        return pl.BlockSpec(array.shape, lambda i: (0,) * array.ndim)

    taps_spec = pl.BlockSpec((3, 3, width), lambda i: (0, 0, i))
    hbm = pl.BlockSpec(memory_space=pltpu.HBM)
    vmem = pl.BlockSpec(memory_space=pltpu.VMEM)
    params = pltpu.CompilerParams(vmem_limit_bytes=32 * MIB)
    keep = functools.partial(pltpu.with_memory_space_constraint, memory_space=pltpu.HBM)
    key_plain, value_plain = key_proj, value_proj
    query_proj, key_proj, value_proj = keep(query_proj), keep(key_proj), keep(value_proj)
    swap = [(i, i ^ 1) for i in range(devices)]

    heads, tails, outer = pl.pallas_call(
        edge_kernel,
        in_specs=[hbm, hbm, hbm],
        out_specs=[vmem] * 3,
        out_shape=[pltpu.VMEM((8, channels), BF16)] * 3,
        scratch_shapes=[pltpu.VMEM((6, 16, channels), BF16), pltpu.SemaphoreType.DMA((6,))],
        compiler_params=params,
        name="edges",
    )(query_proj, key_proj, value_proj)
    between = [(i - 1, i) for i in range(2, devices, 2)]
    between += [(i, i - 1) for i in range(2, devices, 2) if shift_of(i // 2)]
    outer = lax.ppermute(outer, "ctx", between)

    near_sums, inner = pl.pallas_call(
        functools.partial(moment_kernel, width=width),
        in_specs=[vmem, vmem] + [vmem] * 4,
        out_specs=[vmem, vmem],
        out_shape=[pltpu.VMEM((RANK, channels), F32), pltpu.VMEM((4 * RANK, channels), BF16)],
        compiler_params=params,
        cost_estimate=pl.CostEstimate(
            flops=1, bytes_accessed=1, transcendentals=0
        ),
        name="moments",
    )(heads, tails, key_plain, value_plain, short_filter, moment)
    inner, outer = lax.optimization_barrier((inner, outer))
    inner = lax.ppermute(inner, "ctx", swap)
    outer_more = lax.ppermute(outer, "ctx", swap)

    sent, side = pl.pallas_call(
        merge_kernel,
        in_specs=[vmem] * 9,
        out_specs=[hbm, vmem],
        out_shape=[
            pltpu.HBM((devices // 2 * RANK, channels), BF16),
            pltpu.VMEM((2 * RANK, channels), F32),
        ],
        scratch_shapes=[pltpu.VMEM((16, channels), BF16), pltpu.SemaphoreType.DMA((devices // 2 * RANK // 16,))],
        compiler_params=params,
        name="merge",
    )(heads, tails, inner, outer, outer_more, near_sums, short_filter, first, widen)

    groups = [[2 * chip + core for chip in chip_order(devices // 2)] for core in range(2)]
    got = lax.all_to_all(sent, "ctx", 0, 0, axis_index_groups=groups, tiled=True)

    local_args = tuple(
        keep(arg)
        for arg in (query_proj, key_proj, value_proj, short_filter, skip_gain.reshape(1, -1), pole_rates.T,
                    pole_residues.T, mix, toeplitz, near, spread)
    )
    feat, full, local, weight = pl.pallas_call(
        local_kernel,
        in_specs=[vmem] + [hbm] * len(local_args),
        out_specs=[vmem] * 4,
        out_shape=[
            pltpu.VMEM((block, channels), BF16),
            pltpu.VMEM((block, channels), BF16),
            pltpu.VMEM((block, channels), F32),
            pltpu.VMEM((NODES + 8, channels), F32),
        ],
        scratch_shapes=[pltpu.VMEM(arg.shape, arg.dtype) for arg in local_args]
        + [pltpu.VMEM((NODES, width), F32), pltpu.SemaphoreType.DMA((9 + 3 * (channels // width),))],
        compiler_params=params,
        cost_estimate=pl.CostEstimate(
            flops=8 * toeplitz.size * channels, bytes_accessed=16 * block * channels, transcendentals=0
        ),
        name="local",
    )(side, *local_args)

    return pl.pallas_call(
        out_kernel,
        in_specs=[vmem] * 7,
        out_specs=hbm,
        out_shape=pltpu.HBM((block, channels), BF16),
        scratch_shapes=[
            pltpu.VMEM((channels // width, block, width), BF16),
            pltpu.SemaphoreType.DMA((channels // width,)),
        ],
        compiler_params=params,
        name="output",
    )(feat, full, local, weight, got, carry, spread)


def solution(mesh):
    placed = (
        P("ctx", "tp"),
        P("ctx", "tp"),
        P("ctx", "tp"),
        P(None, None, "tp"),
        P("tp"),
        P("tp", None),
        P("tp", None),
    )
    return jax.shard_map(
        on_device, mesh=mesh, in_specs=placed, out_specs=P("ctx", "tp"), check_vma=False
    )
```

```python
import functools

import jax
import jax.numpy as jnp
import ml_dtypes
import numpy as np
from jax import lax
from jax.experimental import pallas as pl
from jax.experimental.pallas import tpu as pltpu
from jax.sharding import PartitionSpec as P

RATE_MIN, RATE_MAX = 0.3 / 4096, 1.0 / 30.0
SHIFT = 1.2e-3
NODES = 24
RANK = 8
PAD = 80
ROW = 4
F32 = jnp.float32
BF16 = jnp.bfloat16
MIB = 1024 * 1024


def split_np(values):
    high = values.astype(np.float32).astype(ml_dtypes.bfloat16)
    low = (values - high.astype(np.float64)).astype(np.float32).astype(ml_dtypes.bfloat16)
    return high, low


def log_range():
    low, high = np.log(RATE_MIN + SHIFT), np.log(RATE_MAX + SHIFT)
    return (low + high) / 2, (high - low) / 2


def basis_of(count):
    rates = np.linspace(RATE_MIN, RATE_MAX, 1500)
    basis = np.linalg.svd(np.exp(-np.outer(rates, np.arange(count))), full_matrices=False)[2][:RANK]
    return basis * np.sign(basis[:, :1])


def shift_of(chip):
    return 0 if chip % ROW == 0 else 2


ORDER = (10, 14, 11, 15, 6, 7, 13, 9, 3, 2, 5, 8, 12, 1, 4, 0)


def chip_order(chips):
    return ORDER if chips == len(ORDER) else tuple(range(chips))


@functools.lru_cache(maxsize=None)
def tables(block, devices):
    mid, half = log_range()
    order = np.arange(NODES)
    node_x = np.cos((2 * order + 1) * np.pi / (2 * NODES))
    nodes = np.exp(mid + half * node_x) - SHIFT
    weights = np.full(NODES, 2.0 / NODES)
    weights[0] = 1.0 / NODES
    to_nodes = np.cos(order[None, :] * np.arccos(node_x)[:, None]) * weights[None, :]

    lags = np.arange(block)
    near, wide = basis_of(block), basis_of(2 * block + 2)
    near_share = np.exp(-np.outer(nodes, lags)) @ near.T
    wide_share = np.exp(-np.outer(nodes, np.arange(2 * block + 2))) @ wide.T
    mix = np.concatenate([to_nodes, near_share.T @ to_nodes], 0).astype(np.float32)

    lag = lags[:, None] - lags[None, :]
    toeplitz = np.where(lag >= 0, near[:, np.maximum(lag, 0)], 0.0).reshape(RANK * block, block)
    toeplitz = np.concatenate(split_np(toeplitz), 1)
    near_back = near[:, ::-1]
    moment = np.concatenate(split_np(near_back), 1)
    first = np.zeros((2 * RANK, 128), np.float32)
    first[:RANK, 0:2] = near_back[:, :2]
    first[RANK:, 0:2] = wide[:, 1::-1]
    widen = [
        np.concatenate([wide[:, by + block : by + 2 * block] @ near.T, wide[:, by : by + block] @ near.T], 1)
        for by in (0, 2)
    ]
    blank = np.zeros_like(widen[0])
    high, low = split_np(np.concatenate([widen[0], blank, widen[1], blank], 0))
    widen = np.concatenate([high, low, high, np.zeros_like(high)], 1)

    chips = devices // 2
    place = np.arange(devices)
    sources = np.array(chip_order(chips))
    starts = np.array([2 * block * (i // 2) + (block if i % 2 else shift_of(i // 2)) for i in place])
    ends = np.array([2 * block * (chip + 1) + shift_of(chip + 1) for chip in sources])
    lead = np.maximum(starts[:, None] - ends[None, :], 0)
    before = (place // 2)[:, None] > sources[None, :]
    decay = np.where(before[:, None, :], np.exp(-nodes[None, :, None] * lead[:, None, :]), 0.0)
    carry = (decay[:, :, :, None] * wide_share[None, :, None, :]).reshape(devices, NODES, chips * RANK)
    carry = np.concatenate(split_np(carry), 1).reshape(devices * 2 * NODES, chips * RANK)

    upper = [np.exp(-np.outer(lags + 1 - by, nodes)) * (lags >= by - 1)[:, None] for by in (0, 1, 2)]
    lower = [np.exp(-np.outer(lags - 1, nodes)), np.zeros((block, NODES)), -np.exp(nodes)[None, :] * (lags == 0)[:, None]]
    spread = []
    for parts in (lower, upper):
        high, low = split_np(np.concatenate(parts + [np.zeros((block, PAD - 3 * NODES))], 1))
        spread.append(np.concatenate([high, low, high], 1))
    spread = np.concatenate(spread, 0)
    high, low = split_np(near_share)
    near_share = np.concatenate([high, low, high, np.zeros_like(high)], 1)
    return mix, toeplitz, moment, first, widen, near_share, carry, spread


def split(values):
    high = values.astype(BF16)
    return high, (values - high.astype(F32)).astype(BF16)


def dot(left, right):
    return jnp.dot(left, right, preferred_element_type=F32)


def exact_dot(left, right):
    return jnp.dot(left, right, preferred_element_type=F32, precision=lax.Precision.HIGHEST)


def rounded(values):
    return values.astype(BF16).astype(F32)


def zeros(rows, columns):
    return jnp.zeros((rows, columns), F32)


def edge_kernel(q_ref, k_ref, v_ref, heads_ref, tails_ref, outer_ref, held, sems):
    block, columns = q_ref.shape
    copies = []
    for idx, ref in enumerate((k_ref, v_ref, q_ref)):
        copies.append(pltpu.make_async_copy(ref.at[pl.ds(0, 16)], held.at[idx], sems.at[idx]))
        copies.append(pltpu.make_async_copy(ref.at[pl.ds(block - 16, 16)], held.at[idx + 3], sems.at[idx + 3]))
    for copy in copies:
        copy.start()
    for copy in copies:
        copy.wait()
    heads = [held[idx].astype(F32)[0:2] for idx in range(3)]
    tails = [held[idx + 3].astype(F32)[14:16] for idx in range(3)]
    heads = jnp.concatenate(heads + [zeros(2, columns)], 0)
    tails = jnp.concatenate(tails + [zeros(2, columns)], 0)
    heads_ref[...] = heads.astype(BF16)
    tails_ref[...] = tails.astype(BF16)
    outer_ref[...] = jnp.where(lax.rem(lax.axis_index("ctx"), 2) == 0, heads, tails).astype(BF16)


def featurize(values, taps):
    row = lax.broadcasted_iota(jnp.int32, values.shape, 0)
    one = jnp.where(row < 1, 0.0, pltpu.roll(values, 1, 0))
    two = jnp.where(row < 2, 0.0, pltpu.roll(values, 2, 0))
    return rounded(taps[0:1] * values + taps[1:2] * one + taps[2:3] * two)


def moment_kernel(heads_ref, tails_ref, k_ref, v_ref, taps_ref, moment_ref, near_ref, inner_ref, *, width):
    block, columns = k_ref.shape
    steps = columns // width
    row = lax.broadcasted_iota(jnp.int32, (block, width), 0)
    for step in range(steps):
        cols = slice(step * width, (step + 1) * width)
        key_feat = featurize(k_ref[:, cols].astype(F32), taps_ref[1, :, cols])
        value_feat = featurize(v_ref[:, cols].astype(F32), taps_ref[2, :, cols])
        product = jnp.where(row < 2, 0.0, key_feat * value_feat).astype(BF16)
        near = dot(moment_ref[...], jnp.concatenate([product, product], 0))
        near_ref[:, cols] = near
        rows = [tails_ref[:, cols].astype(F32), heads_ref[:, cols].astype(F32), zeros(8, width)]
        inner_ref[:, cols] = jnp.concatenate([near] + rows, 0).astype(BF16)


def two_rows(head, tail, taps):
    row0 = taps[0:1] * head[0:1] + taps[1:2] * tail[1:2] + taps[2:3] * tail[0:1]
    row1 = taps[0:1] * head[1:2] + taps[1:2] * head[0:1] + taps[2:3] * tail[1:2]
    return rounded(row0), rounded(row1)


def product_rows(heads, tails, taps_ref):
    key = two_rows(heads[0:2], tails[0:2], taps_ref[1])
    value = two_rows(heads[2:4], tails[2:4], taps_ref[2])
    return rounded(key[0] * value[0]), rounded(key[1] * value[1])


def merge_kernel(heads_ref, tails_ref, inner_ref, outer_ref, outer_more_ref, near_ref, taps_ref, first_ref, widen_ref,
                 sent_ref, side_ref, held, sems):
    place = lax.axis_index("ctx")
    lower = lax.rem(place, 2) == 0
    chip = lax.div(place, 2)
    opens, closes = lax.rem(chip, ROW) == 0, lax.rem(chip + 1, ROW) == 0
    heads, tails, inner = heads_ref[...].astype(F32)[0:4], tails_ref[...].astype(F32)[0:4], inner_ref[...].astype(F32)
    outer, outer_more = outer_ref[...].astype(F32), outer_more_ref[...].astype(F32)
    tails_other, heads_other = inner[8:12], inner[16:20]
    heads0, heads1 = jnp.where(lower, heads, heads_other), jnp.where(lower, heads_other, heads)
    tails0, tails1 = jnp.where(lower, tails, tails_other), jnp.where(lower, tails_other, tails)
    outer0, outer1 = jnp.where(lower, outer, outer_more), jnp.where(lower, outer_more, outer)
    a0, a1 = product_rows(heads0, outer0[0:4], taps_ref)
    b0, b1 = product_rows(heads1, tails0, taps_ref)
    c0, c1 = (jnp.where(closes, 0.0, row) for row in product_rows(outer1[0:4], tails1, taps_ref))
    near, near_other = near_ref[...], inner[:RANK]
    first, last = first_ref[:RANK], first_ref[RANK:]
    near0 = jnp.where(lower, near, near_other)
    near0 += jnp.where(opens, first[:, 0:1] * a0 + first[:, 1:2] * a1, 0.0)
    near1 = jnp.where(lower, near_other, near) + first[:, 0:1] * b0 + first[:, 1:2] * b1
    high, low = split(jnp.concatenate([near0, near1], 0))
    widen = widen_ref[pl.ds(pl.multiple_of(jnp.where(closes, 0, 2 * RANK), 2 * RANK), 2 * RANK)]
    whole = dot(widen, jnp.concatenate([high, high, low, jnp.zeros_like(low)], 0))[:RANK]
    whole += last[:, 0:1] * c0 + last[:, 1:2] * c1
    held[...] = jnp.concatenate([whole, whole], 0).astype(BF16)
    copies = [
        pltpu.make_async_copy(held, sent_ref.at[pl.ds(idx * 16, 16)], sems.at[idx])
        for idx in range(sent_ref.shape[0] // 16)
    ]
    for copy in copies:
        copy.start()
    rows = [jnp.where(lower, a0, b0), jnp.where(lower, a1, b1), jnp.where(lower, outer[4:6], inner[12:14])]
    rows += [zeros(4, a0.shape[1]), jnp.where(lower, 0.0, near0)]
    side_ref[...] = jnp.concatenate(rows, 0)
    for copy in copies:
        copy.wait()


def spread_start(block):
    place = lax.axis_index("ctx")
    plain = jnp.logical_or(lax.rem(place, 2) == 1, lax.rem(lax.div(place, 2), ROW) == 0)
    return pl.multiple_of(jnp.where(plain, block, 0), block)


def local_kernel(side_ref, q_hbm, k_hbm, v_hbm, taps_hbm, skip_hbm, rates_hbm, residues_hbm, mix_hbm, toeplitz_hbm,
                 near_hbm, spread_hbm, feat_ref, full_ref, local_ref, weight_ref, q_ref, k_ref, v_ref, taps_ref,
                 skip_ref, rates_ref, residues_ref, mix_ref, toeplitz_ref, near_ref, spread_ref, cheb_ref, sems):
    block, channels = q_ref.shape
    width = 512
    steps = channels // width
    count = 0

    def load(source, target):
        nonlocal count
        copy = pltpu.make_async_copy(source, target, sems.at[count])
        copy.start()
        count += 1
        return copy

    filters = [load(rates_hbm, rates_ref), load(residues_hbm, residues_ref), load(mix_hbm, mix_ref),
               load(skip_hbm, skip_ref)]
    rows = [load(taps_hbm, taps_ref), load(near_hbm, near_ref)]
    signals = []
    for step in range(steps):
        at = (slice(None), pl.ds(step * width, width))
        signals.append([load(k_hbm.at[at], k_ref.at[at]), load(v_hbm.at[at], v_ref.at[at])])
        if step == 0:
            matrices = [load(spread_hbm, spread_ref), load(toeplitz_hbm, toeplitz_ref)]
    queries = []
    for step in range(steps):
        at = (slice(None), pl.ds(step * width, width))
        queries.append(load(q_hbm.at[at], q_ref.at[at]))

    mid, half = log_range()
    kind = spread_start(block)
    row = lax.broadcasted_iota(jnp.int32, (block, width), 0)
    for copy in filters:
        copy.wait()
    for step in range(steps):
        cols = slice(step * width, (step + 1) * width)
        x = (jnp.log(rates_ref[:, cols] + SHIFT) - mid) * (1.0 / half)
        before = residues_ref[:, cols]
        now = before * x
        cheb_ref[0:1, cols] = jnp.sum(before, 0, keepdims=True)
        cheb_ref[1:2, cols] = jnp.sum(now, 0, keepdims=True)
        twice = 2.0 * x
        for order in range(2, NODES):
            before, now = now, twice * now - before
            cheb_ref[order : order + 1, cols] = jnp.sum(now, 0, keepdims=True)
    mixed = exact_dot(mix_ref[...], cheb_ref[...])
    weight = mixed[:NODES]
    weight_ref[...] = jnp.concatenate([weight, skip_ref[...], zeros(7, channels)], 0)
    for copy in rows:
        copy.wait()
    side = side_ref[...]
    row0, row1, edge = side[0:1], side[1:2], side[2:4]
    high, low = split(side[8:])
    state = dot(near_ref[...], jnp.concatenate([high, high, low, jnp.zeros_like(low)], 0))
    stacked = jnp.concatenate(
        [weight * state, weight * row0, weight * row1, zeros(PAD - 3 * NODES, channels)], 0
    )
    high, low = split(stacked)
    stacked = jnp.concatenate([high, high, low], 0)
    for copy in matrices:
        copy.wait()
    spread = spread_ref[pl.ds(kind, block)]

    for step in range(steps):
        cols = slice(step * width, (step + 1) * width)
        for copy in signals[step]:
            copy.wait()
        product = featurize(k_ref[:, cols].astype(F32), taps_ref[1, :, cols]) * featurize(
            v_ref[:, cols].astype(F32), taps_ref[2, :, cols]
        )
        full_ref[:, cols] = jnp.where(
            row == 0, row0[:, cols], jnp.where(row == 1, row1[:, cols], product)
        ).astype(BF16)
        product = jnp.where(row < 2, 0.0, product).astype(BF16)
        twin = jnp.concatenate([product, product], 0)
        for part in range(width // 256):
            inner = slice(part * 256, part * 256 + 256)
            outer = slice(step * width + part * 256, step * width + part * 256 + 256)
            total = dot(spread, stacked[:, outer])
            for k in range(RANK):
                total += mixed[NODES + k : NODES + k + 1, outer] * dot(
                    toeplitz_ref[k * block : (k + 1) * block], twin[:, inner]
                )
            local_ref[:, outer] = total

        queries[step].wait()
        values = q_ref[:, cols].astype(F32)
        taps = taps_ref[0, :, cols]
        one = jnp.where(row == 0, edge[1:2, cols], pltpu.roll(values, 1, 0))
        two = jnp.where(row == 0, edge[0:1, cols], jnp.where(row == 1, edge[1:2, cols], pltpu.roll(values, 2, 0)))
        feat_ref[:, cols] = (taps[0:1] * values + taps[1:2] * one + taps[2:3] * two).astype(BF16)


def out_kernel(feat_ref, full_ref, local_ref, weight_ref, got_ref, carry_ref, spread_ref, out_ref, held, sems):
    place = lax.axis_index("ctx")
    carry = carry_ref[pl.ds(pl.multiple_of(place * 2 * NODES, 2 * NODES), 2 * NODES)]
    _, block, width = held.shape
    spread = spread_ref[pl.ds(spread_start(block), block)]
    state = dot(carry, got_ref[...])
    state = weight_ref[:NODES] * (state[:NODES] + state[NODES:])
    high, low = split(jnp.concatenate([state, zeros(PAD - NODES, state.shape[1])], 0))
    stacked = jnp.concatenate([high, high, low], 0)
    copies = []
    for step in range(held.shape[0]):
        cols = slice(step * width, (step + 1) * width)
        convolved = local_ref[:, cols] + dot(spread, stacked[:, cols])
        skip = weight_ref[NODES : NODES + 1, cols]
        held[step] = (
            feat_ref[:, cols].astype(F32) * (rounded(convolved) + skip * full_ref[:, cols].astype(F32))
        ).astype(BF16)
        copies.append(pltpu.make_async_copy(held.at[step], out_ref.at[:, pl.ds(step * width, width)], sems.at[step]))
        copies[-1].start()
    for copy in copies:
        copy.wait()


def on_device(query_proj, key_proj, value_proj, short_filter, skip_gain, pole_rates, pole_residues):
    block, channels = query_proj.shape
    devices = lax.axis_size("ctx")
    poles = pole_rates.shape[1]
    mix, toeplitz, moment, first, widen, near, carry, spread = (jnp.asarray(table) for table in tables(block, devices))
    width = 512
    grid = (channels // width,)

    def cols(rows):
        return pl.BlockSpec((rows, width), lambda i: (0, i))

    def fixed(array):
        return pl.BlockSpec(array.shape, lambda i: (0,) * array.ndim)

    taps_spec = pl.BlockSpec((3, 3, width), lambda i: (0, 0, i))
    hbm = pl.BlockSpec(memory_space=pltpu.HBM)
    vmem = pl.BlockSpec(memory_space=pltpu.VMEM)
    params = pltpu.CompilerParams(vmem_limit_bytes=32 * MIB)
    keep = functools.partial(pltpu.with_memory_space_constraint, memory_space=pltpu.HBM)
    key_plain, value_plain = key_proj, value_proj
    query_proj, key_proj, value_proj = keep(query_proj), keep(key_proj), keep(value_proj)
    swap = [(i, i ^ 1) for i in range(devices)]

    heads, tails, outer = pl.pallas_call(
        edge_kernel,
        in_specs=[hbm, hbm, hbm],
        out_specs=[vmem] * 3,
        out_shape=[pltpu.VMEM((8, channels), BF16)] * 3,
        scratch_shapes=[pltpu.VMEM((6, 16, channels), BF16), pltpu.SemaphoreType.DMA((6,))],
        compiler_params=params,
        name="edges",
    )(query_proj, key_proj, value_proj)
    between = [(i - 1, i) for i in range(2, devices, 2)]
    between += [(i, i - 1) for i in range(2, devices, 2) if shift_of(i // 2)]
    outer = lax.ppermute(outer, "ctx", between)

    near_sums, inner = pl.pallas_call(
        functools.partial(moment_kernel, width=width),
        in_specs=[vmem, vmem] + [vmem] * 4,
        out_specs=[vmem, vmem],
        out_shape=[pltpu.VMEM((RANK, channels), F32), pltpu.VMEM((4 * RANK, channels), BF16)],
        compiler_params=params,
        cost_estimate=pl.CostEstimate(
            flops=1, bytes_accessed=1, transcendentals=0
        ),
        name="moments",
    )(heads, tails, key_plain, value_plain, short_filter, moment)
    inner, outer = lax.optimization_barrier((inner, outer))
    inner = lax.ppermute(inner, "ctx", swap)
    outer_more = lax.ppermute(outer, "ctx", swap)

    sent, side = pl.pallas_call(
        merge_kernel,
        in_specs=[vmem] * 9,
        out_specs=[hbm, vmem],
        out_shape=[
            pltpu.HBM((devices // 2 * RANK, channels), BF16),
            pltpu.VMEM((2 * RANK, channels), F32),
        ],
        scratch_shapes=[pltpu.VMEM((16, channels), BF16), pltpu.SemaphoreType.DMA((devices // 2 * RANK // 16,))],
        compiler_params=params,
        name="merge",
    )(heads, tails, inner, outer, outer_more, near_sums, short_filter, first, widen)

    groups = [[2 * chip + core for chip in chip_order(devices // 2)] for core in range(2)]
    got = lax.all_to_all(sent, "ctx", 0, 0, axis_index_groups=groups, tiled=True)

    local_args = tuple(
        keep(arg)
        for arg in (query_proj, key_proj, value_proj, short_filter, skip_gain.reshape(1, -1), pole_rates.T,
                    pole_residues.T, mix, toeplitz, near, spread)
    )
    feat, full, local, weight = pl.pallas_call(
        local_kernel,
        in_specs=[vmem] + [hbm] * len(local_args),
        out_specs=[vmem] * 4,
        out_shape=[
            pltpu.VMEM((block, channels), BF16),
            pltpu.VMEM((block, channels), BF16),
            pltpu.VMEM((block, channels), F32),
            pltpu.VMEM((NODES + 8, channels), F32),
        ],
        scratch_shapes=[pltpu.VMEM(arg.shape, arg.dtype) for arg in local_args]
        + [pltpu.VMEM((NODES, channels), F32), pltpu.SemaphoreType.DMA((9 + 3 * (channels // width),))],
        compiler_params=params,
        cost_estimate=pl.CostEstimate(
            flops=8 * toeplitz.size * channels, bytes_accessed=16 * block * channels, transcendentals=0
        ),
        name="local",
    )(side, *local_args)

    return pl.pallas_call(
        out_kernel,
        in_specs=[vmem] * 7,
        out_specs=hbm,
        out_shape=pltpu.HBM((block, channels), BF16),
        scratch_shapes=[
            pltpu.VMEM((channels // width, block, width), BF16),
            pltpu.SemaphoreType.DMA((channels // width,)),
        ],
        compiler_params=params,
        name="output",
    )(feat, full, local, weight, got, carry, spread)


def solution(mesh):
    placed = (
        P("ctx", "tp"),
        P("ctx", "tp"),
        P("ctx", "tp"),
        P(None, None, "tp"),
        P("tp"),
        P("tp", None),
        P("tp", None),
    )
    return jax.shard_map(
        on_device, mesh=mesh, in_specs=placed, out_specs=P("ctx", "tp"), check_vma=False
    )
```

```python
import functools

import jax
import jax.numpy as jnp
import ml_dtypes
import numpy as np
from jax import lax
from jax.experimental import pallas as pl
from jax.experimental.pallas import tpu as pltpu
from jax.sharding import PartitionSpec as P

RATE_MIN, RATE_MAX = 0.3 / 4096, 1.0 / 30.0
SHIFT = 1.2e-3
NODES = 24
RANK = 8
PAD = 80
ROW = 4
F32 = jnp.float32
BF16 = jnp.bfloat16
MIB = 1024 * 1024


def split_np(values):
    high = values.astype(np.float32).astype(ml_dtypes.bfloat16)
    low = (values - high.astype(np.float64)).astype(np.float32).astype(ml_dtypes.bfloat16)
    return high, low


def log_range():
    low, high = np.log(RATE_MIN + SHIFT), np.log(RATE_MAX + SHIFT)
    return (low + high) / 2, (high - low) / 2


def basis_of(count):
    rates = np.linspace(RATE_MIN, RATE_MAX, 1500)
    basis = np.linalg.svd(np.exp(-np.outer(rates, np.arange(count))), full_matrices=False)[2][:RANK]
    return basis * np.sign(basis[:, :1])


def shift_of(chip):
    return 0 if chip % ROW == 0 else 2


ORDER = (10, 14, 11, 15, 6, 7, 13, 9, 3, 2, 5, 8, 12, 1, 4, 0)


def chip_order(chips):
    return ORDER if chips == len(ORDER) else tuple(range(chips))


@functools.lru_cache(maxsize=None)
def tables(block, devices):
    mid, half = log_range()
    order = np.arange(NODES)
    node_x = np.cos((2 * order + 1) * np.pi / (2 * NODES))
    nodes = np.exp(mid + half * node_x) - SHIFT
    weights = np.full(NODES, 2.0 / NODES)
    weights[0] = 1.0 / NODES
    to_nodes = np.cos(order[None, :] * np.arccos(node_x)[:, None]) * weights[None, :]

    lags = np.arange(block)
    near, wide = basis_of(block), basis_of(2 * block + 2)
    near_share = np.exp(-np.outer(nodes, lags)) @ near.T
    wide_share = np.exp(-np.outer(nodes, np.arange(2 * block + 2))) @ wide.T
    mix = np.concatenate([to_nodes, near_share.T @ to_nodes], 0).astype(np.float32)

    lag = lags[:, None] - lags[None, :]
    toeplitz = np.where(lag >= 0, near[:, np.maximum(lag, 0)], 0.0).reshape(RANK * block, block)
    toeplitz = np.concatenate(split_np(toeplitz), 1)
    near_back = near[:, ::-1]
    moment = np.concatenate(split_np(near_back), 1)
    first = np.zeros((2 * RANK, 128), np.float32)
    first[:RANK, 0:2] = near_back[:, :2]
    first[RANK:, 0:2] = wide[:, 1::-1]
    widen = [
        np.concatenate([wide[:, by + block : by + 2 * block] @ near.T, wide[:, by : by + block] @ near.T], 1)
        for by in (0, 2)
    ]
    blank = np.zeros_like(widen[0])
    high, low = split_np(np.concatenate([widen[0], blank, widen[1], blank], 0))
    widen = np.concatenate([high, low, high, np.zeros_like(high)], 1)

    chips = devices // 2
    place = np.arange(devices)
    sources = np.array(chip_order(chips))
    starts = np.array([2 * block * (i // 2) + (block if i % 2 else shift_of(i // 2)) for i in place])
    ends = np.array([2 * block * (chip + 1) + shift_of(chip + 1) for chip in sources])
    lead = np.maximum(starts[:, None] - ends[None, :], 0)
    before = (place // 2)[:, None] > sources[None, :]
    decay = np.where(before[:, None, :], np.exp(-nodes[None, :, None] * lead[:, None, :]), 0.0)
    carry = (decay[:, :, :, None] * wide_share[None, :, None, :]).reshape(devices, NODES, chips * RANK)
    carry = np.concatenate(split_np(carry), 1).reshape(devices * 2 * NODES, chips * RANK)

    upper = [np.exp(-np.outer(lags + 1 - by, nodes)) * (lags >= by - 1)[:, None] for by in (0, 1, 2)]
    lower = [np.exp(-np.outer(lags - 1, nodes)), np.zeros((block, NODES)), -np.exp(nodes)[None, :] * (lags == 0)[:, None]]
    spread = []
    for parts in (lower, upper):
        high, low = split_np(np.concatenate(parts + [np.zeros((block, PAD - 3 * NODES))], 1))
        spread.append(np.concatenate([high, low, high], 1))
    spread = np.concatenate(spread, 0)
    high, low = split_np(near_share)
    near_share = np.concatenate([high, low, high, np.zeros_like(high)], 1)
    return mix, toeplitz, moment, first, widen, near_share, carry, spread


def split(values):
    high = values.astype(BF16)
    return high, (values - high.astype(F32)).astype(BF16)


def dot(left, right):
    return jnp.dot(left, right, preferred_element_type=F32)


def exact_dot(left, right):
    return jnp.dot(left, right, preferred_element_type=F32, precision=lax.Precision.HIGHEST)


def rounded(values):
    return values.astype(BF16).astype(F32)


def zeros(rows, columns):
    return jnp.zeros((rows, columns), F32)


def edge_kernel(q_ref, k_ref, v_ref, heads_ref, tails_ref, outer_ref, held, sems):
    block, columns = q_ref.shape
    copies = []
    for idx, ref in enumerate((k_ref, v_ref, q_ref)):
        copies.append(pltpu.make_async_copy(ref.at[pl.ds(0, 16)], held.at[idx], sems.at[idx]))
        copies.append(pltpu.make_async_copy(ref.at[pl.ds(block - 16, 16)], held.at[idx + 3], sems.at[idx + 3]))
    for copy in copies:
        copy.start()
    for copy in copies:
        copy.wait()
    heads = [held[idx].astype(F32)[0:2] for idx in range(3)]
    tails = [held[idx + 3].astype(F32)[14:16] for idx in range(3)]
    heads = jnp.concatenate(heads + [zeros(2, columns)], 0)
    tails = jnp.concatenate(tails + [zeros(2, columns)], 0)
    heads_ref[...] = heads.astype(BF16)
    tails_ref[...] = tails.astype(BF16)
    outer_ref[...] = jnp.where(lax.rem(lax.axis_index("ctx"), 2) == 0, heads, tails).astype(BF16)


def featurize(values, taps):
    row = lax.broadcasted_iota(jnp.int32, values.shape, 0)
    one = jnp.where(row < 1, 0.0, pltpu.roll(values, 1, 0))
    two = jnp.where(row < 2, 0.0, pltpu.roll(values, 2, 0))
    return rounded(taps[0:1] * values + taps[1:2] * one + taps[2:3] * two)


def moment_kernel(heads_ref, tails_ref, k_ref, v_ref, taps_ref, moment_ref, near_ref, inner_ref, *, width):
    block, columns = k_ref.shape
    steps = columns // width
    row = lax.broadcasted_iota(jnp.int32, (block, width), 0)
    for step in range(steps):
        cols = slice(step * width, (step + 1) * width)
        key_feat = featurize(k_ref[:, cols].astype(F32), taps_ref[1, :, cols])
        value_feat = featurize(v_ref[:, cols].astype(F32), taps_ref[2, :, cols])
        product = jnp.where(row < 2, 0.0, key_feat * value_feat).astype(BF16)
        near = dot(moment_ref[...], jnp.concatenate([product, product], 0))
        near_ref[:, cols] = near
        rows = [ref[:, cols].astype(F32)[0:4] for ref in (tails_ref, heads_ref)]
        inner_ref[:, cols] = jnp.concatenate([near] + rows, 0).astype(BF16)


def two_rows(head, tail, taps):
    row0 = taps[0:1] * head[0:1] + taps[1:2] * tail[1:2] + taps[2:3] * tail[0:1]
    row1 = taps[0:1] * head[1:2] + taps[1:2] * head[0:1] + taps[2:3] * tail[1:2]
    return rounded(row0), rounded(row1)


def product_rows(heads, tails, taps_ref):
    key = two_rows(heads[0:2], tails[0:2], taps_ref[1])
    value = two_rows(heads[2:4], tails[2:4], taps_ref[2])
    return rounded(key[0] * value[0]), rounded(key[1] * value[1])


def merge_kernel(heads_ref, tails_ref, tails_other_ref, inner_ref, outer_ref, outer_more_ref, near_ref, taps_ref,
                 first_ref, widen_ref, sent_ref, side_ref, held, sems):
    place = lax.axis_index("ctx")
    lower = lax.rem(place, 2) == 0
    chip = lax.div(place, 2)
    opens, closes = lax.rem(chip, ROW) == 0, lax.rem(chip + 1, ROW) == 0
    heads, tails, inner = heads_ref[...].astype(F32)[0:4], tails_ref[...].astype(F32)[0:4], inner_ref[...].astype(F32)
    outer, outer_more = outer_ref[...].astype(F32), outer_more_ref[...].astype(F32)
    tails_other, heads_other = inner[8:12], inner[12:16]
    heads0, heads1 = jnp.where(lower, heads, heads_other), jnp.where(lower, heads_other, heads)
    tails0, tails1 = jnp.where(lower, tails, tails_other), jnp.where(lower, tails_other, tails)
    outer0, outer1 = jnp.where(lower, outer, outer_more), jnp.where(lower, outer_more, outer)
    a0, a1 = product_rows(heads0, outer0[0:4], taps_ref)
    b0, b1 = product_rows(heads1, tails0, taps_ref)
    c0, c1 = (jnp.where(closes, 0.0, row) for row in product_rows(outer1[0:4], tails1, taps_ref))
    near, near_other = near_ref[...], inner[:RANK]
    first, last = first_ref[:RANK], first_ref[RANK:]
    near0 = jnp.where(lower, near, near_other)
    near0 += jnp.where(opens, first[:, 0:1] * a0 + first[:, 1:2] * a1, 0.0)
    near1 = jnp.where(lower, near_other, near) + first[:, 0:1] * b0 + first[:, 1:2] * b1
    high, low = split(jnp.concatenate([near0, near1], 0))
    widen = widen_ref[pl.ds(pl.multiple_of(jnp.where(closes, 0, 2 * RANK), 2 * RANK), 2 * RANK)]
    whole = dot(widen, jnp.concatenate([high, high, low, jnp.zeros_like(low)], 0))[:RANK]
    whole += last[:, 0:1] * c0 + last[:, 1:2] * c1
    held[...] = jnp.concatenate([whole, whole], 0).astype(BF16)
    copies = [
        pltpu.make_async_copy(held, sent_ref.at[pl.ds(idx * 16, 16)], sems.at[idx])
        for idx in range(sent_ref.shape[0] // 16)
    ]
    for copy in copies:
        copy.start()
    rows = [jnp.where(lower, a0, b0), jnp.where(lower, a1, b1), jnp.where(lower, outer[4:6], tails_other_ref[...].astype(F32)[4:6])]
    rows += [zeros(4, a0.shape[1]), jnp.where(lower, 0.0, near0)]
    side_ref[...] = jnp.concatenate(rows, 0)
    for copy in copies:
        copy.wait()


def spread_start(block):
    place = lax.axis_index("ctx")
    plain = jnp.logical_or(lax.rem(place, 2) == 1, lax.rem(lax.div(place, 2), ROW) == 0)
    return pl.multiple_of(jnp.where(plain, block, 0), block)


def local_kernel(side_ref, q_hbm, k_hbm, v_hbm, taps_hbm, skip_hbm, rates_hbm, residues_hbm, mix_hbm, toeplitz_hbm,
                 near_hbm, spread_hbm, feat_ref, full_ref, local_ref, weight_ref, q_ref, k_ref, v_ref, taps_ref,
                 skip_ref, rates_ref, residues_ref, mix_ref, toeplitz_ref, near_ref, spread_ref, cheb_ref, sems):
    block, channels = q_ref.shape
    width = 512
    steps = channels // width
    count = 0

    def load(source, target):
        nonlocal count
        copy = pltpu.make_async_copy(source, target, sems.at[count])
        copy.start()
        count += 1
        return copy

    filters = [load(rates_hbm, rates_ref), load(residues_hbm, residues_ref), load(mix_hbm, mix_ref),
               load(skip_hbm, skip_ref)]
    rows = [load(taps_hbm, taps_ref), load(near_hbm, near_ref)]
    signals = []
    for step in range(steps):
        at = (slice(None), pl.ds(step * width, width))
        signals.append([load(k_hbm.at[at], k_ref.at[at]), load(v_hbm.at[at], v_ref.at[at])])
        if step == 0:
            matrices = [load(spread_hbm, spread_ref), load(toeplitz_hbm, toeplitz_ref)]
    queries = []
    for step in range(steps):
        at = (slice(None), pl.ds(step * width, width))
        queries.append(load(q_hbm.at[at], q_ref.at[at]))

    mid, half = log_range()
    kind = spread_start(block)
    row = lax.broadcasted_iota(jnp.int32, (block, width), 0)
    for copy in filters:
        copy.wait()
    for step in range(steps):
        cols = slice(step * width, (step + 1) * width)
        x = (jnp.log(rates_ref[:, cols] + SHIFT) - mid) * (1.0 / half)
        before = residues_ref[:, cols]
        now = before * x
        cheb_ref[0:1, cols] = jnp.sum(before, 0, keepdims=True)
        cheb_ref[1:2, cols] = jnp.sum(now, 0, keepdims=True)
        twice = 2.0 * x
        for order in range(2, NODES):
            before, now = now, twice * now - before
            cheb_ref[order : order + 1, cols] = jnp.sum(now, 0, keepdims=True)
    mixed = exact_dot(mix_ref[...], cheb_ref[...])
    weight = mixed[:NODES]
    weight_ref[...] = jnp.concatenate([weight, skip_ref[...], zeros(7, channels)], 0)
    for copy in rows:
        copy.wait()
    side = side_ref[...]
    row0, row1, edge = side[0:1], side[1:2], side[2:4]
    high, low = split(side[8:])
    state = dot(near_ref[...], jnp.concatenate([high, high, low, jnp.zeros_like(low)], 0))
    stacked = jnp.concatenate(
        [weight * state, weight * row0, weight * row1, zeros(PAD - 3 * NODES, channels)], 0
    )
    high, low = split(stacked)
    stacked = jnp.concatenate([high, high, low], 0)
    for copy in matrices:
        copy.wait()
    spread = spread_ref[pl.ds(kind, block)]

    for step in range(steps):
        cols = slice(step * width, (step + 1) * width)
        for copy in signals[step]:
            copy.wait()
        product = featurize(k_ref[:, cols].astype(F32), taps_ref[1, :, cols]) * featurize(
            v_ref[:, cols].astype(F32), taps_ref[2, :, cols]
        )
        full_ref[:, cols] = jnp.where(
            row == 0, row0[:, cols], jnp.where(row == 1, row1[:, cols], product)
        ).astype(BF16)
        product = jnp.where(row < 2, 0.0, product).astype(BF16)
        twin = jnp.concatenate([product, product], 0)
        for part in range(width // 256):
            inner = slice(part * 256, part * 256 + 256)
            outer = slice(step * width + part * 256, step * width + part * 256 + 256)
            total = dot(spread, stacked[:, outer])
            for k in range(RANK):
                total += mixed[NODES + k : NODES + k + 1, outer] * dot(
                    toeplitz_ref[k * block : (k + 1) * block], twin[:, inner]
                )
            local_ref[:, outer] = total

        queries[step].wait()
        values = q_ref[:, cols].astype(F32)
        taps = taps_ref[0, :, cols]
        one = jnp.where(row == 0, edge[1:2, cols], pltpu.roll(values, 1, 0))
        two = jnp.where(row == 0, edge[0:1, cols], jnp.where(row == 1, edge[1:2, cols], pltpu.roll(values, 2, 0)))
        feat_ref[:, cols] = (taps[0:1] * values + taps[1:2] * one + taps[2:3] * two).astype(BF16)


def out_kernel(feat_ref, full_ref, local_ref, weight_ref, got_ref, carry_ref, spread_ref, out_ref, held, sems):
    place = lax.axis_index("ctx")
    carry = carry_ref[pl.ds(pl.multiple_of(place * 2 * NODES, 2 * NODES), 2 * NODES)]
    _, block, width = held.shape
    spread = spread_ref[pl.ds(spread_start(block), block)]
    state = dot(carry, got_ref[...])
    state = weight_ref[:NODES] * (state[:NODES] + state[NODES:])
    high, low = split(jnp.concatenate([state, zeros(PAD - NODES, state.shape[1])], 0))
    stacked = jnp.concatenate([high, high, low], 0)
    copies = []
    for step in range(held.shape[0]):
        cols = slice(step * width, (step + 1) * width)
        convolved = local_ref[:, cols] + dot(spread, stacked[:, cols])
        skip = weight_ref[NODES : NODES + 1, cols]
        held[step] = (
            feat_ref[:, cols].astype(F32) * (rounded(convolved) + skip * full_ref[:, cols].astype(F32))
        ).astype(BF16)
        copies.append(pltpu.make_async_copy(held.at[step], out_ref.at[:, pl.ds(step * width, width)], sems.at[step]))
        copies[-1].start()
    for copy in copies:
        copy.wait()


def on_device(query_proj, key_proj, value_proj, short_filter, skip_gain, pole_rates, pole_residues):
    block, channels = query_proj.shape
    devices = lax.axis_size("ctx")
    poles = pole_rates.shape[1]
    mix, toeplitz, moment, first, widen, near, carry, spread = (jnp.asarray(table) for table in tables(block, devices))
    width = 512
    grid = (channels // width,)

    def cols(rows):
        return pl.BlockSpec((rows, width), lambda i: (0, i))

    def fixed(array):
        return pl.BlockSpec(array.shape, lambda i: (0,) * array.ndim)

    taps_spec = pl.BlockSpec((3, 3, width), lambda i: (0, 0, i))
    hbm = pl.BlockSpec(memory_space=pltpu.HBM)
    vmem = pl.BlockSpec(memory_space=pltpu.VMEM)
    params = pltpu.CompilerParams(vmem_limit_bytes=32 * MIB)
    keep = functools.partial(pltpu.with_memory_space_constraint, memory_space=pltpu.HBM)
    key_plain, value_plain = key_proj, value_proj
    query_proj, key_proj, value_proj = keep(query_proj), keep(key_proj), keep(value_proj)
    swap = [(i, i ^ 1) for i in range(devices)]

    heads, tails, outer = pl.pallas_call(
        edge_kernel,
        in_specs=[hbm, hbm, hbm],
        out_specs=[vmem] * 3,
        out_shape=[pltpu.VMEM((8, channels), BF16)] * 3,
        scratch_shapes=[pltpu.VMEM((6, 16, channels), BF16), pltpu.SemaphoreType.DMA((6,))],
        compiler_params=params,
        name="edges",
    )(query_proj, key_proj, value_proj)
    between = [(i - 1, i) for i in range(2, devices, 2)]
    between += [(i, i - 1) for i in range(2, devices, 2) if shift_of(i // 2)]
    outer = lax.ppermute(outer, "ctx", between)

    near_sums, inner = pl.pallas_call(
        functools.partial(moment_kernel, width=width),
        in_specs=[vmem, vmem] + [vmem] * 4,
        out_specs=[vmem, vmem],
        out_shape=[pltpu.VMEM((RANK, channels), F32), pltpu.VMEM((2 * RANK, channels), BF16)],
        compiler_params=params,
        cost_estimate=pl.CostEstimate(
            flops=1, bytes_accessed=1, transcendentals=0
        ),
        name="moments",
    )(heads, tails, key_plain, value_plain, short_filter, moment)
    inner = lax.ppermute(inner, "ctx", swap)
    outer_more = lax.ppermute(outer, "ctx", swap)
    tails_other = lax.ppermute(tails, "ctx", swap)

    sent, side = pl.pallas_call(
        merge_kernel,
        in_specs=[vmem] * 10,
        out_specs=[hbm, vmem],
        out_shape=[
            pltpu.HBM((devices // 2 * RANK, channels), BF16),
            pltpu.VMEM((2 * RANK, channels), F32),
        ],
        scratch_shapes=[pltpu.VMEM((16, channels), BF16), pltpu.SemaphoreType.DMA((devices // 2 * RANK // 16,))],
        compiler_params=params,
        name="merge",
    )(heads, tails, tails_other, inner, outer, outer_more, near_sums, short_filter, first, widen)

    groups = [[2 * chip + core for chip in chip_order(devices // 2)] for core in range(2)]
    got = lax.all_to_all(sent, "ctx", 0, 0, axis_index_groups=groups, tiled=True)

    local_args = tuple(
        keep(arg)
        for arg in (query_proj, key_proj, value_proj, short_filter, skip_gain.reshape(1, -1), pole_rates.T,
                    pole_residues.T, mix, toeplitz, near, spread)
    )
    feat, full, local, weight = pl.pallas_call(
        local_kernel,
        in_specs=[vmem] + [hbm] * len(local_args),
        out_specs=[vmem] * 4,
        out_shape=[
            pltpu.VMEM((block, channels), BF16),
            pltpu.VMEM((block, channels), BF16),
            pltpu.VMEM((block, channels), F32),
            pltpu.VMEM((NODES + 8, channels), F32),
        ],
        scratch_shapes=[pltpu.VMEM(arg.shape, arg.dtype) for arg in local_args]
        + [pltpu.VMEM((NODES, channels), F32), pltpu.SemaphoreType.DMA((9 + 3 * (channels // width),))],
        compiler_params=params,
        cost_estimate=pl.CostEstimate(
            flops=8 * toeplitz.size * channels, bytes_accessed=16 * block * channels, transcendentals=0
        ),
        name="local",
    )(side, *local_args)

    return pl.pallas_call(
        out_kernel,
        in_specs=[vmem] * 7,
        out_specs=hbm,
        out_shape=pltpu.HBM((block, channels), BF16),
        scratch_shapes=[
            pltpu.VMEM((channels // width, block, width), BF16),
            pltpu.SemaphoreType.DMA((channels // width,)),
        ],
        compiler_params=params,
        name="output",
    )(feat, full, local, weight, got, carry, spread)


def solution(mesh):
    placed = (
        P("ctx", "tp"),
        P("ctx", "tp"),
        P("ctx", "tp"),
        P(None, None, "tp"),
        P("tp"),
        P("tp", None),
        P("tp", None),
    )
    return jax.shard_map(
        on_device, mesh=mesh, in_specs=placed, out_specs=P("ctx", "tp"), check_vma=False
    )
```

```python
import functools

import jax
import jax.numpy as jnp
import ml_dtypes
import numpy as np
from jax import lax
from jax.experimental import pallas as pl
from jax.experimental.pallas import tpu as pltpu
from jax.sharding import PartitionSpec as P

RATE_MIN, RATE_MAX = 0.3 / 4096, 1.0 / 30.0
SHIFT = 1.2e-3
NODES = 24
RANK = 8
PAD = 80
ROW = 4
F32 = jnp.float32
BF16 = jnp.bfloat16
MIB = 1024 * 1024


def split_np(values):
    high = values.astype(np.float32).astype(ml_dtypes.bfloat16)
    low = (values - high.astype(np.float64)).astype(np.float32).astype(ml_dtypes.bfloat16)
    return high, low


def log_range():
    low, high = np.log(RATE_MIN + SHIFT), np.log(RATE_MAX + SHIFT)
    return (low + high) / 2, (high - low) / 2


def basis_of(count):
    rates = np.linspace(RATE_MIN, RATE_MAX, 1500)
    basis = np.linalg.svd(np.exp(-np.outer(rates, np.arange(count))), full_matrices=False)[2][:RANK]
    return basis * np.sign(basis[:, :1])


def shift_of(chip):
    return 0 if chip % ROW == 0 else 2


ORDER = (10, 14, 11, 15, 6, 7, 13, 9, 3, 2, 5, 8, 12, 1, 4, 0)


def chip_order(chips):
    return ORDER if chips == len(ORDER) else tuple(range(chips))


@functools.lru_cache(maxsize=None)
def tables(block, devices):
    mid, half = log_range()
    order = np.arange(NODES)
    node_x = np.cos((2 * order + 1) * np.pi / (2 * NODES))
    nodes = np.exp(mid + half * node_x) - SHIFT
    weights = np.full(NODES, 2.0 / NODES)
    weights[0] = 1.0 / NODES
    to_nodes = np.cos(order[None, :] * np.arccos(node_x)[:, None]) * weights[None, :]

    lags = np.arange(block)
    near, wide = basis_of(block), basis_of(2 * block + 2)
    near_share = np.exp(-np.outer(nodes, lags)) @ near.T
    wide_share = np.exp(-np.outer(nodes, np.arange(2 * block + 2))) @ wide.T
    mix = np.concatenate([to_nodes, near_share.T @ to_nodes], 0).astype(np.float32)

    lag = lags[:, None] - lags[None, :]
    toeplitz = np.where(lag >= 0, near[:, np.maximum(lag, 0)], 0.0).reshape(RANK * block, block)
    toeplitz = np.concatenate(split_np(toeplitz), 1)
    near_back = near[:, ::-1]
    moment = np.concatenate(split_np(near_back), 1)
    first = np.zeros((2 * RANK, 128), np.float32)
    first[:RANK, 0:2] = near_back[:, :2]
    first[RANK:, 0:2] = wide[:, 1::-1]
    widen = [
        np.concatenate([wide[:, by + block : by + 2 * block] @ near.T, wide[:, by : by + block] @ near.T], 1)
        for by in (0, 2)
    ]
    blank = np.zeros_like(widen[0])
    high, low = split_np(np.concatenate([widen[0], blank, widen[1], blank], 0))
    widen = np.concatenate([high, low, high, np.zeros_like(high)], 1)

    chips = devices // 2
    place = np.arange(devices)
    sources = np.array(chip_order(chips))
    starts = np.array([2 * block * (i // 2) + (block if i % 2 else shift_of(i // 2)) for i in place])
    ends = np.array([2 * block * (chip + 1) + shift_of(chip + 1) for chip in sources])
    lead = np.maximum(starts[:, None] - ends[None, :], 0)
    before = (place // 2)[:, None] > sources[None, :]
    decay = np.where(before[:, None, :], np.exp(-nodes[None, :, None] * lead[:, None, :]), 0.0)
    carry = (decay[:, :, :, None] * wide_share[None, :, None, :]).reshape(devices, NODES, chips * RANK)
    carry = np.concatenate(split_np(carry), 1).reshape(devices * 2 * NODES, chips * RANK)

    upper = [np.exp(-np.outer(lags + 1 - by, nodes)) * (lags >= by - 1)[:, None] for by in (0, 1, 2)]
    lower = [np.exp(-np.outer(lags - 1, nodes)), np.zeros((block, NODES)), -np.exp(nodes)[None, :] * (lags == 0)[:, None]]
    spread = []
    for parts in (lower, upper):
        high, low = split_np(np.concatenate(parts + [np.zeros((block, PAD - 3 * NODES))], 1))
        spread.append(np.concatenate([high, low, high], 1))
    spread = np.concatenate(spread, 0)
    high, low = split_np(near_share)
    near_share = np.concatenate([high, low, high, np.zeros_like(high)], 1)
    return mix, toeplitz, moment, first, widen, near_share, carry, spread


def split(values):
    high = values.astype(BF16)
    return high, (values - high.astype(F32)).astype(BF16)


def dot(left, right):
    return jnp.dot(left, right, preferred_element_type=F32)


def exact_dot(left, right):
    return jnp.dot(left, right, preferred_element_type=F32, precision=lax.Precision.HIGHEST)


def rounded(values):
    return values.astype(BF16).astype(F32)


def zeros(rows, columns):
    return jnp.zeros((rows, columns), F32)


def edge_kernel(q_ref, k_ref, v_ref, heads_ref, tails_ref, outer_ref, held, sems):
    block, columns = q_ref.shape
    copies = [
        pltpu.make_async_copy(ref.at[pl.ds(start, 16)], held.at[idx], sems.at[idx])
        for idx, (ref, start) in enumerate(
            ((k_ref, 0), (v_ref, 0), (k_ref, block - 16), (v_ref, block - 16), (q_ref, block - 16))
        )
    ]
    for copy in copies:
        copy.start()
    for copy in copies:
        copy.wait()
    heads = [held[idx].astype(F32)[0:2] for idx in range(2)]
    tails = [held[idx].astype(F32)[14:16] for idx in range(2, 5)]
    heads = jnp.concatenate(heads + [zeros(4, columns)], 0)
    tails = jnp.concatenate(tails + [zeros(2, columns)], 0)
    heads_ref[...] = heads.astype(BF16)
    tails_ref[...] = tails.astype(BF16)
    outer_ref[...] = jnp.where(lax.rem(lax.axis_index("ctx"), 2) == 0, heads, tails).astype(BF16)


def featurize(values, taps):
    row = lax.broadcasted_iota(jnp.int32, values.shape, 0)
    one = jnp.where(row < 1, 0.0, pltpu.roll(values, 1, 0))
    two = jnp.where(row < 2, 0.0, pltpu.roll(values, 2, 0))
    return rounded(taps[0:1] * values + taps[1:2] * one + taps[2:3] * two)


def moment_kernel(heads_ref, tails_ref, k_ref, v_ref, taps_ref, moment_ref, near_ref, inner_ref, *, width):
    block, columns = k_ref.shape
    steps = columns // width
    row = lax.broadcasted_iota(jnp.int32, (block, width), 0)
    for step in range(steps):
        cols = slice(step * width, (step + 1) * width)
        key_feat = featurize(k_ref[:, cols].astype(F32), taps_ref[1, :, cols])
        value_feat = featurize(v_ref[:, cols].astype(F32), taps_ref[2, :, cols])
        product = jnp.where(row < 2, 0.0, key_feat * value_feat).astype(BF16)
        near = dot(moment_ref[...], jnp.concatenate([product, product], 0))
        near_ref[:, cols] = near
        rows = [ref[:, cols].astype(F32)[0:4] for ref in (tails_ref, heads_ref)]
        inner_ref[:, cols] = jnp.concatenate([near] + rows, 0).astype(BF16)


def two_rows(head, tail, taps):
    row0 = taps[0:1] * head[0:1] + taps[1:2] * tail[1:2] + taps[2:3] * tail[0:1]
    row1 = taps[0:1] * head[1:2] + taps[1:2] * head[0:1] + taps[2:3] * tail[1:2]
    return rounded(row0), rounded(row1)


def product_rows(heads, tails, taps_ref):
    key = two_rows(heads[0:2], tails[0:2], taps_ref[1])
    value = two_rows(heads[2:4], tails[2:4], taps_ref[2])
    return rounded(key[0] * value[0]), rounded(key[1] * value[1])


def merge_kernel(heads_ref, tails_ref, tails_other_ref, inner_ref, outer_ref, outer_more_ref, near_ref, taps_ref,
                 first_ref, widen_ref, sent_ref, side_ref, held, sems):
    place = lax.axis_index("ctx")
    lower = lax.rem(place, 2) == 0
    chip = lax.div(place, 2)
    opens, closes = lax.rem(chip, ROW) == 0, lax.rem(chip + 1, ROW) == 0
    heads, tails, inner = heads_ref[...].astype(F32)[0:4], tails_ref[...].astype(F32)[0:4], inner_ref[...].astype(F32)
    outer, outer_more = outer_ref[...].astype(F32), outer_more_ref[...].astype(F32)
    tails_other, heads_other = inner[8:12], inner[12:16]
    heads0, heads1 = jnp.where(lower, heads, heads_other), jnp.where(lower, heads_other, heads)
    tails0, tails1 = jnp.where(lower, tails, tails_other), jnp.where(lower, tails_other, tails)
    outer0, outer1 = jnp.where(lower, outer, outer_more), jnp.where(lower, outer_more, outer)
    a0, a1 = product_rows(heads0, outer0[0:4], taps_ref)
    b0, b1 = product_rows(heads1, tails0, taps_ref)
    c0, c1 = (jnp.where(closes, 0.0, row) for row in product_rows(outer1[0:4], tails1, taps_ref))
    near, near_other = near_ref[...], inner[:RANK]
    first, last = first_ref[:RANK], first_ref[RANK:]
    near0 = jnp.where(lower, near, near_other)
    near0 += jnp.where(opens, first[:, 0:1] * a0 + first[:, 1:2] * a1, 0.0)
    near1 = jnp.where(lower, near_other, near) + first[:, 0:1] * b0 + first[:, 1:2] * b1
    high, low = split(jnp.concatenate([near0, near1], 0))
    widen = widen_ref[pl.ds(pl.multiple_of(jnp.where(closes, 0, 2 * RANK), 2 * RANK), 2 * RANK)]
    whole = dot(widen, jnp.concatenate([high, high, low, jnp.zeros_like(low)], 0))[:RANK]
    whole += last[:, 0:1] * c0 + last[:, 1:2] * c1
    held[...] = jnp.concatenate([whole, whole], 0).astype(BF16)
    copies = [
        pltpu.make_async_copy(held, sent_ref.at[pl.ds(idx * 16, 16)], sems.at[idx])
        for idx in range(sent_ref.shape[0] // 16)
    ]
    for copy in copies:
        copy.start()
    rows = [jnp.where(lower, a0, b0), jnp.where(lower, a1, b1), jnp.where(lower, outer[4:6], tails_other_ref[...].astype(F32)[4:6])]
    rows += [zeros(4, a0.shape[1]), jnp.where(lower, 0.0, near0)]
    side_ref[...] = jnp.concatenate(rows, 0)
    for copy in copies:
        copy.wait()


def spread_start(block):
    place = lax.axis_index("ctx")
    plain = jnp.logical_or(lax.rem(place, 2) == 1, lax.rem(lax.div(place, 2), ROW) == 0)
    return pl.multiple_of(jnp.where(plain, block, 0), block)


def local_kernel(side_ref, q_hbm, k_hbm, v_hbm, taps_hbm, skip_hbm, rates_hbm, residues_hbm, mix_hbm, toeplitz_hbm,
                 near_hbm, spread_hbm, feat_ref, full_ref, local_ref, weight_ref, q_ref, k_ref, v_ref, taps_ref,
                 skip_ref, rates_ref, residues_ref, mix_ref, toeplitz_ref, near_ref, spread_ref, cheb_ref, sems):
    block, channels = q_ref.shape
    width = 512
    steps = channels // width
    count = 0

    def load(source, target):
        nonlocal count
        copy = pltpu.make_async_copy(source, target, sems.at[count])
        copy.start()
        count += 1
        return copy

    filters = [load(rates_hbm, rates_ref), load(residues_hbm, residues_ref), load(mix_hbm, mix_ref),
               load(skip_hbm, skip_ref)]
    rows = [load(taps_hbm, taps_ref), load(near_hbm, near_ref)]
    signals = []
    for step in range(steps):
        at = (slice(None), pl.ds(step * width, width))
        signals.append([load(k_hbm.at[at], k_ref.at[at]), load(v_hbm.at[at], v_ref.at[at])])
        if step == 0:
            matrices = [load(spread_hbm, spread_ref), load(toeplitz_hbm, toeplitz_ref)]
    queries = []
    for step in range(steps):
        at = (slice(None), pl.ds(step * width, width))
        queries.append(load(q_hbm.at[at], q_ref.at[at]))

    mid, half = log_range()
    kind = spread_start(block)
    row = lax.broadcasted_iota(jnp.int32, (block, width), 0)
    for copy in filters:
        copy.wait()
    for step in range(steps):
        cols = slice(step * width, (step + 1) * width)
        x = (jnp.log(rates_ref[:, cols] + SHIFT) - mid) * (1.0 / half)
        before = residues_ref[:, cols]
        now = before * x
        cheb_ref[0:1, cols] = jnp.sum(before, 0, keepdims=True)
        cheb_ref[1:2, cols] = jnp.sum(now, 0, keepdims=True)
        twice = 2.0 * x
        for order in range(2, NODES):
            before, now = now, twice * now - before
            cheb_ref[order : order + 1, cols] = jnp.sum(now, 0, keepdims=True)
    mixed = exact_dot(mix_ref[...], cheb_ref[...])
    weight = mixed[:NODES]
    weight_ref[...] = jnp.concatenate([weight, skip_ref[...], zeros(7, channels)], 0)
    for copy in rows:
        copy.wait()
    side = side_ref[...]
    row0, row1, edge = side[0:1], side[1:2], side[2:4]
    high, low = split(side[8:])
    state = dot(near_ref[...], jnp.concatenate([high, high, low, jnp.zeros_like(low)], 0))
    stacked = jnp.concatenate(
        [weight * state, weight * row0, weight * row1, zeros(PAD - 3 * NODES, channels)], 0
    )
    high, low = split(stacked)
    stacked = jnp.concatenate([high, high, low], 0)
    for copy in matrices:
        copy.wait()
    spread = spread_ref[pl.ds(kind, block)]

    for step in range(steps):
        cols = slice(step * width, (step + 1) * width)
        for copy in signals[step]:
            copy.wait()
        product = featurize(k_ref[:, cols].astype(F32), taps_ref[1, :, cols]) * featurize(
            v_ref[:, cols].astype(F32), taps_ref[2, :, cols]
        )
        full_ref[:, cols] = jnp.where(
            row == 0, row0[:, cols], jnp.where(row == 1, row1[:, cols], product)
        ).astype(BF16)
        product = jnp.where(row < 2, 0.0, product).astype(BF16)
        twin = jnp.concatenate([product, product], 0)
        for part in range(width // 256):
            inner = slice(part * 256, part * 256 + 256)
            outer = slice(step * width + part * 256, step * width + part * 256 + 256)
            total = dot(spread, stacked[:, outer])
            for k in range(RANK):
                total += mixed[NODES + k : NODES + k + 1, outer] * dot(
                    toeplitz_ref[k * block : (k + 1) * block], twin[:, inner]
                )
            local_ref[:, outer] = total

        queries[step].wait()
        values = q_ref[:, cols].astype(F32)
        taps = taps_ref[0, :, cols]
        one = jnp.where(row == 0, edge[1:2, cols], pltpu.roll(values, 1, 0))
        two = jnp.where(row == 0, edge[0:1, cols], jnp.where(row == 1, edge[1:2, cols], pltpu.roll(values, 2, 0)))
        feat_ref[:, cols] = (taps[0:1] * values + taps[1:2] * one + taps[2:3] * two).astype(BF16)


def out_kernel(feat_ref, full_ref, local_ref, weight_ref, got_ref, carry_ref, spread_ref, out_ref, held, sems):
    place = lax.axis_index("ctx")
    carry = carry_ref[pl.ds(pl.multiple_of(place * 2 * NODES, 2 * NODES), 2 * NODES)]
    _, block, width = held.shape
    spread = spread_ref[pl.ds(spread_start(block), block)]
    state = dot(carry, got_ref[...])
    state = weight_ref[:NODES] * (state[:NODES] + state[NODES:])
    high, low = split(jnp.concatenate([state, zeros(PAD - NODES, state.shape[1])], 0))
    stacked = jnp.concatenate([high, high, low], 0)
    copies = []
    for step in range(held.shape[0]):
        cols = slice(step * width, (step + 1) * width)
        convolved = local_ref[:, cols] + dot(spread, stacked[:, cols])
        skip = weight_ref[NODES : NODES + 1, cols]
        held[step] = (
            feat_ref[:, cols].astype(F32) * (rounded(convolved) + skip * full_ref[:, cols].astype(F32))
        ).astype(BF16)
        copies.append(pltpu.make_async_copy(held.at[step], out_ref.at[:, pl.ds(step * width, width)], sems.at[step]))
        copies[-1].start()
    for copy in copies:
        copy.wait()


def on_device(query_proj, key_proj, value_proj, short_filter, skip_gain, pole_rates, pole_residues):
    block, channels = query_proj.shape
    devices = lax.axis_size("ctx")
    poles = pole_rates.shape[1]
    mix, toeplitz, moment, first, widen, near, carry, spread = (jnp.asarray(table) for table in tables(block, devices))
    width = 512
    grid = (channels // width,)

    def cols(rows):
        return pl.BlockSpec((rows, width), lambda i: (0, i))

    def fixed(array):
        return pl.BlockSpec(array.shape, lambda i: (0,) * array.ndim)

    taps_spec = pl.BlockSpec((3, 3, width), lambda i: (0, 0, i))
    hbm = pl.BlockSpec(memory_space=pltpu.HBM)
    vmem = pl.BlockSpec(memory_space=pltpu.VMEM)
    params = pltpu.CompilerParams(vmem_limit_bytes=32 * MIB)
    keep = functools.partial(pltpu.with_memory_space_constraint, memory_space=pltpu.HBM)
    key_plain, value_plain = key_proj, value_proj
    query_proj, key_proj, value_proj = keep(query_proj), keep(key_proj), keep(value_proj)
    swap = [(i, i ^ 1) for i in range(devices)]

    heads, tails, outer = pl.pallas_call(
        edge_kernel,
        in_specs=[hbm, hbm, hbm],
        out_specs=[vmem] * 3,
        out_shape=[pltpu.VMEM((8, channels), BF16)] * 3,
        scratch_shapes=[pltpu.VMEM((5, 16, channels), BF16), pltpu.SemaphoreType.DMA((5,))],
        compiler_params=params,
        name="edges",
    )(query_proj, key_proj, value_proj)
    between = [(i - 1, i) for i in range(2, devices, 2)]
    between += [(i, i - 1) for i in range(2, devices, 2) if shift_of(i // 2)]
    outer = lax.ppermute(outer, "ctx", between)

    near_sums, inner = pl.pallas_call(
        functools.partial(moment_kernel, width=width),
        in_specs=[vmem, vmem] + [vmem] * 4,
        out_specs=[vmem, vmem],
        out_shape=[pltpu.VMEM((RANK, channels), F32), pltpu.VMEM((2 * RANK, channels), BF16)],
        compiler_params=params,
        cost_estimate=pl.CostEstimate(
            flops=1, bytes_accessed=1, transcendentals=0
        ),
        name="moments",
    )(heads, tails, key_plain, value_plain, short_filter, moment)
    inner = lax.ppermute(inner, "ctx", swap)
    outer_more = lax.ppermute(outer, "ctx", swap)
    tails_other = lax.ppermute(tails, "ctx", swap)

    sent, side = pl.pallas_call(
        merge_kernel,
        in_specs=[vmem] * 10,
        out_specs=[hbm, vmem],
        out_shape=[
            pltpu.HBM((devices // 2 * RANK, channels), BF16),
            pltpu.VMEM((2 * RANK, channels), F32),
        ],
        scratch_shapes=[pltpu.VMEM((16, channels), BF16), pltpu.SemaphoreType.DMA((devices // 2 * RANK // 16,))],
        compiler_params=params,
        name="merge",
    )(heads, tails, tails_other, inner, outer, outer_more, near_sums, short_filter, first, widen)

    groups = [[2 * chip + core for chip in chip_order(devices // 2)] for core in range(2)]
    got = lax.all_to_all(sent, "ctx", 0, 0, axis_index_groups=groups, tiled=True)

    local_args = tuple(
        keep(arg)
        for arg in (query_proj, key_proj, value_proj, short_filter, skip_gain.reshape(1, -1), pole_rates.T,
                    pole_residues.T, mix, toeplitz, near, spread)
    )
    feat, full, local, weight = pl.pallas_call(
        local_kernel,
        in_specs=[vmem] + [hbm] * len(local_args),
        out_specs=[vmem] * 4,
        out_shape=[
            pltpu.VMEM((block, channels), BF16),
            pltpu.VMEM((block, channels), BF16),
            pltpu.VMEM((block, channels), F32),
            pltpu.VMEM((NODES + 8, channels), F32),
        ],
        scratch_shapes=[pltpu.VMEM(arg.shape, arg.dtype) for arg in local_args]
        + [pltpu.VMEM((NODES, channels), F32), pltpu.SemaphoreType.DMA((9 + 3 * (channels // width),))],
        compiler_params=params,
        cost_estimate=pl.CostEstimate(
            flops=8 * toeplitz.size * channels, bytes_accessed=16 * block * channels, transcendentals=0
        ),
        name="local",
    )(side, *local_args)

    return pl.pallas_call(
        out_kernel,
        in_specs=[vmem] * 7,
        out_specs=hbm,
        out_shape=pltpu.HBM((block, channels), BF16),
        scratch_shapes=[
            pltpu.VMEM((channels // width, block, width), BF16),
            pltpu.SemaphoreType.DMA((channels // width,)),
        ],
        compiler_params=params,
        name="output",
    )(feat, full, local, weight, got, carry, spread)


def solution(mesh):
    placed = (
        P("ctx", "tp"),
        P("ctx", "tp"),
        P("ctx", "tp"),
        P(None, None, "tp"),
        P("tp"),
        P("tp", None),
        P("tp", None),
    )
    return jax.shard_map(
        on_device, mesh=mesh, in_specs=placed, out_specs=P("ctx", "tp"), check_vma=False
    )
```

```python
import functools

import jax
import jax.numpy as jnp
import ml_dtypes
import numpy as np
from jax import lax
from jax.experimental import pallas as pl
from jax.experimental.pallas import tpu as pltpu
from jax.sharding import PartitionSpec as P

RATE_MIN, RATE_MAX = 0.3 / 4096, 1.0 / 30.0
SHIFT = 1.2e-3
NODES = 24
RANK = 8
PAD = 80
ROW = 4
F32 = jnp.float32
BF16 = jnp.bfloat16
MIB = 1024 * 1024


def split_np(values):
    high = values.astype(np.float32).astype(ml_dtypes.bfloat16)
    low = (values - high.astype(np.float64)).astype(np.float32).astype(ml_dtypes.bfloat16)
    return high, low


def log_range():
    low, high = np.log(RATE_MIN + SHIFT), np.log(RATE_MAX + SHIFT)
    return (low + high) / 2, (high - low) / 2


def basis_of(count):
    rates = np.linspace(RATE_MIN, RATE_MAX, 1500)
    basis = np.linalg.svd(np.exp(-np.outer(rates, np.arange(count))), full_matrices=False)[2][:RANK]
    return basis * np.sign(basis[:, :1])


def shift_of(chip):
    return 0 if chip % ROW == 0 else 2


ORDER = (10, 14, 11, 15, 6, 7, 13, 9, 3, 2, 5, 8, 12, 1, 4, 0)


def chip_order(chips):
    return ORDER if chips == len(ORDER) else tuple(range(chips))


@functools.lru_cache(maxsize=None)
def tables(block, devices):
    mid, half = log_range()
    order = np.arange(NODES)
    node_x = np.cos((2 * order + 1) * np.pi / (2 * NODES))
    nodes = np.exp(mid + half * node_x) - SHIFT
    weights = np.full(NODES, 2.0 / NODES)
    weights[0] = 1.0 / NODES
    to_nodes = np.cos(order[None, :] * np.arccos(node_x)[:, None]) * weights[None, :]

    lags = np.arange(block)
    near, wide = basis_of(block), basis_of(2 * block + 2)
    near_share = np.exp(-np.outer(nodes, lags)) @ near.T
    wide_share = np.exp(-np.outer(nodes, np.arange(2 * block + 2))) @ wide.T
    mix = np.concatenate([to_nodes, near_share.T @ to_nodes], 0).astype(np.float32)

    lag = lags[:, None] - lags[None, :]
    toeplitz = np.where(lag >= 0, near[:, np.maximum(lag, 0)], 0.0).reshape(RANK * block, block)
    toeplitz = np.concatenate(split_np(toeplitz), 1)
    near_back = near[:, ::-1]
    moment = np.concatenate(split_np(near_back), 1)
    first = np.zeros((2 * RANK, 128), np.float32)
    first[:RANK, 0:2] = near_back[:, :2]
    first[RANK:, 0:2] = wide[:, 1::-1]
    widen = [
        np.concatenate([wide[:, by + block : by + 2 * block] @ near.T, wide[:, by : by + block] @ near.T], 1)
        for by in (0, 2)
    ]
    blank = np.zeros_like(widen[0])
    high, low = split_np(np.concatenate([widen[0], blank, widen[1], blank], 0))
    widen = np.concatenate([high, low, high, np.zeros_like(high)], 1)

    chips = devices // 2
    place = np.arange(devices)
    sources = np.array(chip_order(chips))
    starts = np.array([2 * block * (i // 2) + (block if i % 2 else shift_of(i // 2)) for i in place])
    ends = np.array([2 * block * (chip + 1) + shift_of(chip + 1) for chip in sources])
    lead = np.maximum(starts[:, None] - ends[None, :], 0)
    before = (place // 2)[:, None] > sources[None, :]
    decay = np.where(before[:, None, :], np.exp(-nodes[None, :, None] * lead[:, None, :]), 0.0)
    carry = (decay[:, :, :, None] * wide_share[None, :, None, :]).reshape(devices, NODES, chips * RANK)
    carry = np.concatenate(split_np(carry), 1).reshape(devices * 2 * NODES, chips * RANK)

    upper = [np.exp(-np.outer(lags + 1 - by, nodes)) * (lags >= by - 1)[:, None] for by in (0, 1, 2)]
    lower = [np.exp(-np.outer(lags - 1, nodes)), np.zeros((block, NODES)), -np.exp(nodes)[None, :] * (lags == 0)[:, None]]
    spread = []
    for parts in (lower, upper):
        high, low = split_np(np.concatenate(parts + [np.zeros((block, PAD - 3 * NODES))], 1))
        spread.append(np.concatenate([high, low, high], 1))
    spread = np.concatenate(spread, 0)
    high, low = split_np(near_share)
    near_share = np.concatenate([high, low, high, np.zeros_like(high)], 1)
    return mix, toeplitz, moment, first, widen, near_share, carry, spread


def split(values):
    high = values.astype(BF16)
    return high, (values - high.astype(F32)).astype(BF16)


def dot(left, right):
    return jnp.dot(left, right, preferred_element_type=F32)


def exact_dot(left, right):
    return jnp.dot(left, right, preferred_element_type=F32, precision=lax.Precision.HIGHEST)


def rounded(values):
    return values.astype(BF16).astype(F32)


def zeros(rows, columns):
    return jnp.zeros((rows, columns), F32)


def edge_kernel(q_ref, k_ref, v_ref, heads_ref, tails_ref, outer_ref, held, sems):
    block, columns = q_ref.shape
    copies = [
        pltpu.make_async_copy(ref.at[pl.ds(start, 16)], held.at[idx], sems.at[idx])
        for idx, (ref, start) in enumerate(
            ((k_ref, 0), (v_ref, 0), (k_ref, block - 16), (v_ref, block - 16), (q_ref, block - 16))
        )
    ]
    for copy in copies:
        copy.start()
    for copy in copies:
        copy.wait()
    heads = [held[idx].astype(F32)[0:2] for idx in range(2)]
    tails = [held[idx].astype(F32)[14:16] for idx in range(2, 5)]
    heads = jnp.concatenate(heads + [zeros(4, columns)], 0)
    tails = jnp.concatenate(tails + [zeros(2, columns)], 0)
    heads_ref[...] = heads.astype(BF16)
    tails_ref[...] = tails.astype(BF16)
    outer_ref[...] = jnp.where(lax.rem(lax.axis_index("ctx"), 2) == 0, heads, tails).astype(BF16)


def featurize(values, taps):
    row = lax.broadcasted_iota(jnp.int32, values.shape, 0)
    one = jnp.where(row < 1, 0.0, pltpu.roll(values, 1, 0))
    two = jnp.where(row < 2, 0.0, pltpu.roll(values, 2, 0))
    return rounded(taps[0:1] * values + taps[1:2] * one + taps[2:3] * two)


def moment_kernel(heads_ref, tails_ref, k_ref, v_ref, taps_ref, moment_ref, near_ref, inner_ref, *, width):
    block, columns = k_ref.shape
    steps = columns // width
    row = lax.broadcasted_iota(jnp.int32, (block, width), 0)
    for step in range(steps):
        cols = slice(step * width, (step + 1) * width)
        key_feat = featurize(k_ref[:, cols].astype(F32), taps_ref[1, :, cols])
        value_feat = featurize(v_ref[:, cols].astype(F32), taps_ref[2, :, cols])
        product = jnp.where(row < 2, 0.0, key_feat * value_feat).astype(BF16)
        near = dot(moment_ref[...], jnp.concatenate([product, product], 0))
        near_ref[:, cols] = near
        rows = [ref[:, cols].astype(F32)[0:4] for ref in (tails_ref, heads_ref)]
        inner_ref[:, cols] = jnp.concatenate([near] + rows, 0).astype(BF16)


def two_rows(head, tail, taps):
    row0 = taps[0:1] * head[0:1] + taps[1:2] * tail[1:2] + taps[2:3] * tail[0:1]
    row1 = taps[0:1] * head[1:2] + taps[1:2] * head[0:1] + taps[2:3] * tail[1:2]
    return rounded(row0), rounded(row1)


def product_rows(heads, tails, taps_ref):
    key = two_rows(heads[0:2], tails[0:2], taps_ref[1])
    value = two_rows(heads[2:4], tails[2:4], taps_ref[2])
    return rounded(key[0] * value[0]), rounded(key[1] * value[1])


def merge_kernel(heads_ref, tails_ref, tails_other_ref, inner_ref, outer_ref, outer_more_ref, near_ref, taps_ref,
                 first_ref, widen_ref, sent_ref, side_ref, held, sems):
    place = lax.axis_index("ctx")
    lower = lax.rem(place, 2) == 0
    chip = lax.div(place, 2)
    opens, closes = lax.rem(chip, ROW) == 0, lax.rem(chip + 1, ROW) == 0
    heads, tails, inner = heads_ref[...].astype(F32)[0:4], tails_ref[...].astype(F32)[0:4], inner_ref[...].astype(F32)
    outer, outer_more = outer_ref[...].astype(F32), outer_more_ref[...].astype(F32)
    tails_other, heads_other = inner[8:12], inner[12:16]
    heads0, heads1 = jnp.where(lower, heads, heads_other), jnp.where(lower, heads_other, heads)
    tails0, tails1 = jnp.where(lower, tails, tails_other), jnp.where(lower, tails_other, tails)
    outer0, outer1 = jnp.where(lower, outer, outer_more), jnp.where(lower, outer_more, outer)
    a0, a1 = product_rows(heads0, outer0[0:4], taps_ref)
    b0, b1 = product_rows(heads1, tails0, taps_ref)
    c0, c1 = (jnp.where(closes, 0.0, row) for row in product_rows(outer1[0:4], tails1, taps_ref))
    near, near_other = near_ref[...], inner[:RANK]
    first, last = first_ref[:RANK], first_ref[RANK:]
    near0 = jnp.where(lower, near, near_other)
    near0 += jnp.where(opens, first[:, 0:1] * a0 + first[:, 1:2] * a1, 0.0)
    near1 = jnp.where(lower, near_other, near) + first[:, 0:1] * b0 + first[:, 1:2] * b1
    high, low = split(jnp.concatenate([near0, near1], 0))
    widen = widen_ref[pl.ds(pl.multiple_of(jnp.where(closes, 0, 2 * RANK), 2 * RANK), 2 * RANK)]
    whole = dot(widen, jnp.concatenate([high, high, low, jnp.zeros_like(low)], 0))[:RANK]
    whole += last[:, 0:1] * c0 + last[:, 1:2] * c1
    held[...] = jnp.concatenate([whole, whole], 0).astype(BF16)
    copies = [
        pltpu.make_async_copy(held, sent_ref.at[pl.ds(idx * 16, 16)], sems.at[idx])
        for idx in range(sent_ref.shape[0] // 16)
    ]
    for copy in copies:
        copy.start()
    rows = [jnp.where(lower, a0, b0), jnp.where(lower, a1, b1), jnp.where(lower, outer[4:6], tails_other_ref[...].astype(F32)[4:6])]
    rows += [zeros(4, a0.shape[1]), jnp.where(lower, 0.0, near0)]
    side_ref[...] = jnp.concatenate(rows, 0)
    for copy in copies:
        copy.wait()


def spread_start(block):
    place = lax.axis_index("ctx")
    plain = jnp.logical_or(lax.rem(place, 2) == 1, lax.rem(lax.div(place, 2), ROW) == 0)
    return pl.multiple_of(jnp.where(plain, block, 0), block)


def local_kernel(side_ref, q_hbm, k_hbm, v_hbm, taps_hbm, skip_hbm, rates_hbm, residues_hbm, mix_hbm, toeplitz_hbm,
                 near_hbm, spread_hbm, feat_ref, full_ref, local_ref, weight_ref, q_ref, k_ref, v_ref, taps_ref,
                 skip_ref, rates_ref, residues_ref, mix_ref, toeplitz_ref, near_ref, spread_ref, cheb_ref, sems):
    block, channels = q_ref.shape
    width = 512
    steps = channels // width
    count = 0

    def load(source, target):
        nonlocal count
        copy = pltpu.make_async_copy(source, target, sems.at[count])
        copy.start()
        count += 1
        return copy

    filters = [load(rates_hbm, rates_ref), load(residues_hbm, residues_ref), load(mix_hbm, mix_ref),
               load(skip_hbm, skip_ref)]
    rows = [load(taps_hbm, taps_ref), load(near_hbm, near_ref)]
    signals = []
    for step in range(steps):
        at = (slice(None), pl.ds(step * width, width))
        signals.append([load(k_hbm.at[at], k_ref.at[at]), load(v_hbm.at[at], v_ref.at[at])])
        if step == 0:
            matrices = [load(spread_hbm, spread_ref), load(toeplitz_hbm, toeplitz_ref)]
    queries = []
    for step in range(steps):
        at = (slice(None), pl.ds(step * width, width))
        queries.append(load(q_hbm.at[at], q_ref.at[at]))

    mid, half = log_range()
    kind = spread_start(block)
    row = lax.broadcasted_iota(jnp.int32, (block, width), 0)
    for copy in filters:
        copy.wait()
    for step in range(steps):
        cols = slice(step * width, (step + 1) * width)
        x = (jnp.log(rates_ref[:, cols] + SHIFT) - mid) * (1.0 / half)
        before = residues_ref[:, cols]
        now = before * x
        cheb_ref[0:1, cols] = jnp.sum(before, 0, keepdims=True)
        cheb_ref[1:2, cols] = jnp.sum(now, 0, keepdims=True)
        twice = 2.0 * x
        for order in range(2, NODES):
            before, now = now, twice * now - before
            cheb_ref[order : order + 1, cols] = jnp.sum(now, 0, keepdims=True)
    mixed = exact_dot(mix_ref[...], cheb_ref[...])
    weight = mixed[:NODES]
    weight_ref[...] = jnp.concatenate([weight, skip_ref[...], zeros(7, channels)], 0)
    for copy in rows:
        copy.wait()
    side = side_ref[...]
    row0, row1, edge = side[0:1], side[1:2], side[2:4]
    high, low = split(side[8:])
    state = dot(near_ref[...], jnp.concatenate([high, high, low, jnp.zeros_like(low)], 0))
    stacked = jnp.concatenate(
        [weight * state, weight * row0, weight * row1, zeros(PAD - 3 * NODES, channels)], 0
    )
    high, low = split(stacked)
    stacked = jnp.concatenate([high, high, low], 0)
    for copy in matrices:
        copy.wait()
    spread = spread_ref[pl.ds(kind, block)]

    for step in range(steps):
        cols = slice(step * width, (step + 1) * width)
        for copy in signals[step]:
            copy.wait()
        product = featurize(k_ref[:, cols].astype(F32), taps_ref[1, :, cols]) * featurize(
            v_ref[:, cols].astype(F32), taps_ref[2, :, cols]
        )
        full_ref[:, cols] = jnp.where(
            row == 0, row0[:, cols], jnp.where(row == 1, row1[:, cols], product)
        ).astype(BF16)
        product = jnp.where(row < 2, 0.0, product).astype(BF16)
        twin = jnp.concatenate([product, product], 0)
        for part in range(width // 256):
            inner = slice(part * 256, part * 256 + 256)
            outer = slice(step * width + part * 256, step * width + part * 256 + 256)
            total = dot(spread, stacked[:, outer])
            for k in range(RANK):
                total += mixed[NODES + k : NODES + k + 1, outer] * dot(
                    toeplitz_ref[k * block : (k + 1) * block], twin[:, inner]
                )
            local_ref[:, outer] = total

        queries[step].wait()
        values = q_ref[:, cols].astype(F32)
        taps = taps_ref[0, :, cols]
        one = jnp.where(row == 0, edge[1:2, cols], pltpu.roll(values, 1, 0))
        two = jnp.where(row == 0, edge[0:1, cols], jnp.where(row == 1, edge[1:2, cols], pltpu.roll(values, 2, 0)))
        feat_ref[:, cols] = (taps[0:1] * values + taps[1:2] * one + taps[2:3] * two).astype(BF16)


def out_kernel(feat_ref, full_ref, local_ref, weight_ref, got_ref, carry_ref, spread_ref, out_ref, held, sems):
    place = lax.axis_index("ctx")
    carry = carry_ref[pl.ds(pl.multiple_of(place * 2 * NODES, 2 * NODES), 2 * NODES)]
    _, block, width = held.shape
    spread = spread_ref[pl.ds(spread_start(block), block)]
    state = dot(carry, got_ref[...])
    state = weight_ref[:NODES] * (state[:NODES] + state[NODES:])
    high, low = split(jnp.concatenate([state, zeros(PAD - NODES, state.shape[1])], 0))
    stacked = jnp.concatenate([high, high, low], 0)
    copies = []
    for step in range(held.shape[0]):
        cols = slice(step * width, (step + 1) * width)
        convolved = local_ref[:, cols] + dot(spread, stacked[:, cols])
        skip = weight_ref[NODES : NODES + 1, cols]
        held[step] = (
            feat_ref[:, cols].astype(F32) * (rounded(convolved) + skip * full_ref[:, cols].astype(F32))
        ).astype(BF16)
        copies.append(pltpu.make_async_copy(held.at[step], out_ref.at[:, pl.ds(step * width, width)], sems.at[step]))
        copies[-1].start()
    for copy in copies:
        copy.wait()


def on_device(query_proj, key_proj, value_proj, short_filter, skip_gain, pole_rates, pole_residues):
    block, channels = query_proj.shape
    devices = lax.axis_size("ctx")
    poles = pole_rates.shape[1]
    mix, toeplitz, moment, first, widen, near, carry, spread = (jnp.asarray(table) for table in tables(block, devices))
    width = 512
    grid = (channels // width,)

    def cols(rows):
        return pl.BlockSpec((rows, width), lambda i: (0, i))

    def fixed(array):
        return pl.BlockSpec(array.shape, lambda i: (0,) * array.ndim)

    taps_spec = pl.BlockSpec((3, 3, width), lambda i: (0, 0, i))
    hbm = pl.BlockSpec(memory_space=pltpu.HBM)
    vmem = pl.BlockSpec(memory_space=pltpu.VMEM)
    params = pltpu.CompilerParams(vmem_limit_bytes=32 * MIB)
    keep = functools.partial(pltpu.with_memory_space_constraint, memory_space=pltpu.HBM)
    key_plain, value_plain = key_proj, value_proj
    query_proj, key_proj, value_proj = keep(query_proj), keep(key_proj), keep(value_proj)
    swap = [(i, i ^ 1) for i in range(devices)]

    heads, tails, outer = pl.pallas_call(
        edge_kernel,
        in_specs=[hbm, hbm, hbm],
        out_specs=[vmem] * 3,
        out_shape=[pltpu.VMEM((8, channels), BF16)] * 3,
        scratch_shapes=[pltpu.VMEM((5, 16, channels), BF16), pltpu.SemaphoreType.DMA((5,))],
        compiler_params=params,
        name="edges",
    )(query_proj, key_proj, value_proj)
    between = [(i - 1, i) for i in range(2, devices, 2)]
    between += [(i, i - 1) for i in range(2, devices, 2) if shift_of(i // 2)]
    outer = lax.ppermute(outer, "ctx", between)

    near_sums, inner = pl.pallas_call(
        functools.partial(moment_kernel, width=channels // 2),
        in_specs=[vmem, vmem] + [vmem] * 4,
        out_specs=[vmem, vmem],
        out_shape=[pltpu.VMEM((RANK, channels), F32), pltpu.VMEM((2 * RANK, channels), BF16)],
        compiler_params=params,
        cost_estimate=pl.CostEstimate(
            flops=1, bytes_accessed=1, transcendentals=0
        ),
        name="moments",
    )(heads, tails, key_plain, value_plain, short_filter, moment)
    inner = lax.ppermute(inner, "ctx", swap)
    outer_more = lax.ppermute(outer, "ctx", swap)
    tails_other = lax.ppermute(tails, "ctx", swap)

    sent, side = pl.pallas_call(
        merge_kernel,
        in_specs=[vmem] * 10,
        out_specs=[hbm, vmem],
        out_shape=[
            pltpu.HBM((devices // 2 * RANK, channels), BF16),
            pltpu.VMEM((2 * RANK, channels), F32),
        ],
        scratch_shapes=[pltpu.VMEM((16, channels), BF16), pltpu.SemaphoreType.DMA((devices // 2 * RANK // 16,))],
        compiler_params=params,
        name="merge",
    )(heads, tails, tails_other, inner, outer, outer_more, near_sums, short_filter, first, widen)

    groups = [[2 * chip + core for chip in chip_order(devices // 2)] for core in range(2)]
    got = lax.all_to_all(sent, "ctx", 0, 0, axis_index_groups=groups, tiled=True)

    local_args = tuple(
        keep(arg)
        for arg in (query_proj, key_proj, value_proj, short_filter, skip_gain.reshape(1, -1), pole_rates.T,
                    pole_residues.T, mix, toeplitz, near, spread)
    )
    feat, full, local, weight = pl.pallas_call(
        local_kernel,
        in_specs=[vmem] + [hbm] * len(local_args),
        out_specs=[vmem] * 4,
        out_shape=[
            pltpu.VMEM((block, channels), BF16),
            pltpu.VMEM((block, channels), BF16),
            pltpu.VMEM((block, channels), F32),
            pltpu.VMEM((NODES + 8, channels), F32),
        ],
        scratch_shapes=[pltpu.VMEM(arg.shape, arg.dtype) for arg in local_args]
        + [pltpu.VMEM((NODES, channels), F32), pltpu.SemaphoreType.DMA((9 + 3 * (channels // width),))],
        compiler_params=params,
        cost_estimate=pl.CostEstimate(
            flops=8 * toeplitz.size * channels, bytes_accessed=16 * block * channels, transcendentals=0
        ),
        name="local",
    )(side, *local_args)

    return pl.pallas_call(
        out_kernel,
        in_specs=[vmem] * 7,
        out_specs=hbm,
        out_shape=pltpu.HBM((block, channels), BF16),
        scratch_shapes=[
            pltpu.VMEM((channels // width, block, width), BF16),
            pltpu.SemaphoreType.DMA((channels // width,)),
        ],
        compiler_params=params,
        name="output",
    )(feat, full, local, weight, got, carry, spread)


def solution(mesh):
    placed = (
        P("ctx", "tp"),
        P("ctx", "tp"),
        P("ctx", "tp"),
        P(None, None, "tp"),
        P("tp"),
        P("tp", None),
        P("tp", None),
    )
    return jax.shard_map(
        on_device, mesh=mesh, in_specs=placed, out_specs=P("ctx", "tp"), check_vma=False
    )
```
